256 devices in a mesh: dp: 16 (over x, z_lo), seq: 16 (over y, z_hi, core).
Axes of the slice: x: 4, y: 4, z: 8 (z_hi: 2, z_lo: 4; z = z_hi * 4 + z_lo), core: 2. Of those that a mesh axis runs over, the one named last changes fastest.
Arguments:
- frames_in: bfloat16 [16, 4096, 1536], P('dp', 'seq'), may hold values from -6 to 6
- cotangent: bfloat16 [16, 4096, 1536], P('dp', 'seq'), may hold values from -0.09375 to 0.09375
- lengths: int32 [16], P('dp'), may hold values from 1024 to 4096, as said below
- out_weight: bfloat16 [1536, 1536], replicated, may hold values from -0.15625 to 0.15625
- conv_kernel: float32 [32, 1536], replicated, may hold values from -1 to 1
- layer_norm_gain: float32 [1536], replicated, may hold values from 0.5 to 1.5
Outputs:
- input_grad: bfloat16 [16, 4096, 1536], P('dp', 'seq')
- fisher_out: float32 [1536, 1536], P('seq', 'dp')
- fisher_kernel: float32 [32, 1536], P('dp', 'seq')
- fisher_gain: float32 [1536], P('seq')
The draws below stay inside these ranges and needn't reach their ends.
Inputs may be any that keep to these rules, and one draw needn't show every extreme that they name: `lengths`: every recording has at least 1024 valid frames, and at least one recording is valid over all 4096 frames.
All inputs are finite; a program needn't handle non-finite values.
Results may differ from the reference program's by a relative error of at most 0.0049.
Values may be sent and summed in bfloat16 or wider, within the bound.
No kernel may reach another device: no remote copies, remote signals or barrier semaphores. Data moves between devices by JAX's collectives and lax.ppermute only.
A program may use at most 64 MiB of HBM per device.

```python
import jax
import jax.numpy as jnp
from jax import lax

MODEL_WIDTH = 1536
KW = 32
FRAMES = 4096
RECS = 16


def draw_lengths(key, part):
    key = jax.random.fold_in(key, 11)
    first_key, second_key = jax.random.split(key)
    drawn = jax.random.randint(first_key, (RECS,), FRAMES // 4, FRAMES + 1, dtype=jnp.int32)
    chosen = jax.random.randint(second_key, (), 0, RECS, dtype=jnp.int32)
    places = jnp.arange(RECS, dtype=jnp.int32)
    return jnp.where(places == chosen, jnp.int32(FRAMES), drawn).astype(jnp.int32)


def level_of(key, extent, cuts, low, largest):
    factor_of = 1.0
    for dim, blocks in cuts:
        steps = jax.random.uniform(jax.random.fold_in(jax.random.fold_in(key, 6), dim), (blocks,), jnp.float32, low / len(cuts), largest / len(cuts))
        factor_of = factor_of * jnp.repeat(jnp.exp(steps), extent[dim] // blocks).reshape((-1,) + (1,) * (len(extent) - 1 - dim))
    return factor_of


def scatter_about(key, shape, scale, bound, shards=(), kind=jnp.bfloat16):
    gain = level_of(key, shape, shards, -0.22, 0.18) if shards else 1.0
    values = jax.random.normal(key, shape, jnp.float32) * scale * gain
    return jnp.minimum(jnp.maximum(values, -bound), bound).astype(kind)


def setup_inputs(seed: int = 0) -> dict:
    splits = jax.random.split(jax.random.key(seed), 7)
    frames_in = scatter_about(splits[0], (RECS, FRAMES, MODEL_WIDTH), 1.0, 6.0, ((0, 16), (1, 16)))
    cotangent = scatter_about(splits[1], (RECS, FRAMES, MODEL_WIDTH), (FRAMES ** -0.5), 0.09375, ((0, 16), (1, 16)))
    lengths = draw_lengths(jax.random.fold_in(splits[6], 71), 0)
    out_weight = scatter_about(splits[3], (MODEL_WIDTH, MODEL_WIDTH), MODEL_WIDTH ** -0.5, 0.15625)
    conv_kernel = scatter_about(splits[4], (KW, MODEL_WIDTH), KW ** -0.5, 1.0, (), jnp.float32)
    layer_norm_gain = jnp.clip(1.0 + 0.1 * jax.random.normal(splits[5], (MODEL_WIDTH,), jnp.float32), 0.5, 1.5)
    return dict(frames_in=frames_in, cotangent=cotangent, lengths=lengths, out_weight=out_weight, conv_kernel=conv_kernel, layer_norm_gain=layer_norm_gain)


def recording_core(frames_row, cot_row, length, out_weight_g, conv_kernel_g, layer_norm_gain_global):
    frame_total = frames_row.shape[0]
    half_width = KW // 2
    valid_mask = (jnp.arange(frame_total, dtype=jnp.int32) < length).astype(jnp.float32)[:, None]
    masked = (frames_row.astype(jnp.float32) * valid_mask).astype(jnp.bfloat16)
    padded = jnp.pad(masked, ((half_width, half_width), (0, 0))).astype(jnp.float32)
    conv_out = jnp.zeros((frame_total, MODEL_WIDTH), jnp.float32)
    for offset in range(KW):
        conv_out = conv_out + conv_kernel_g[offset] * padded[offset:offset + frame_total]
    row_mean = lax.optimization_barrier(jnp.mean(conv_out, axis=1, keepdims=True))
    centered_input = conv_out - row_mean
    inverse_deviation = lax.rsqrt(lax.optimization_barrier(jnp.mean(centered_input * centered_input, axis=1, keepdims=True)) + 1e-05)
    standardized_input = centered_input * inverse_deviation
    normalized_input = standardized_input * layer_norm_gain_global
    sigma = jax.nn.sigmoid(normalized_input)
    hidden = (normalized_input * sigma).astype(jnp.bfloat16)
    grad_out = (cot_row.astype(jnp.float32) * valid_mask).astype(jnp.bfloat16)
    out_grad = jnp.dot(hidden.T, grad_out, preferred_element_type=jnp.float32)
    hidden_grad = jnp.dot(grad_out, out_weight_g.T, preferred_element_type=jnp.float32)
    normalized_gradient = hidden_grad * (sigma + normalized_input * sigma * (1.0 - sigma))
    gain_gradient = lax.optimization_barrier(jnp.sum(normalized_gradient * standardized_input, axis=0))
    scaled_output = normalized_gradient * layer_norm_gain_global
    convolved_gradient = inverse_deviation * (scaled_output - lax.optimization_barrier(jnp.mean(scaled_output, axis=1, keepdims=True)) - standardized_input * lax.optimization_barrier(jnp.mean(scaled_output * standardized_input, axis=1, keepdims=True)))
    convolved_gradient = convolved_gradient.astype(jnp.bfloat16)
    conv_wide = convolved_gradient.astype(jnp.float32)
    kernel_rows = []
    for offset in range(KW):
        kernel_rows.append(lax.optimization_barrier(jnp.sum(conv_wide * padded[offset:offset + frame_total], axis=0)))
    kernel_grad = jnp.stack(kernel_rows)
    grad_padded = jnp.pad(conv_wide, ((half_width, half_width), (0, 0)))
    summed = jnp.zeros((frame_total, MODEL_WIDTH), jnp.float32)
    for offset in range(KW):
        begin = 2 * half_width - offset
        summed = summed + conv_kernel_g[offset] * grad_padded[begin:begin + frame_total]
    input_grad = (summed * valid_mask).astype(jnp.bfloat16)
    return (input_grad, out_grad, kernel_grad, gain_gradient)

def reference(frames_in, cotangent, lengths, out_weight, conv_kernel, layer_norm_gain):

    def one(items):
        return recording_core(items[0], items[1], items[2], out_weight, conv_kernel, layer_norm_gain)
    input_grad, out_grad, kernel_grad, gain_gradient = lax.map(one, (frames_in, cotangent, lengths))
    count = frames_in.shape[0]
    fisher_out = lax.optimization_barrier(jnp.sum(out_grad * out_grad, axis=0)) / count
    fisher_kernel = lax.optimization_barrier(jnp.sum(kernel_grad * kernel_grad, axis=0)) / count
    fisher_gain = lax.optimization_barrier(jnp.sum(gain_gradient * gain_gradient, axis=0)) / count
    return (input_grad, fisher_out, fisher_kernel, fisher_gain)
```

```python
import jax
import jax.numpy as jnp
from jax import lax
from jax.sharding import PartitionSpec as P

KW = 32
HALF = KW // 2
SEQ = [(y, z, c) for y in range(4) for z in range(2) for c in range(2)]
DP = [(x, z) for x in range(4) for z in range(4)]


def seq_at(y, z, c):
    return ((y % 4) * 2 + z % 2) * 2 + c % 2


def move_y(value, step):
    return lax.ppermute(value, "seq", [(seq_at(*p), seq_at(p[0] + step, p[1], p[2])) for p in SEQ])


def move_z_hi(value):
    return lax.ppermute(value, "seq", [(seq_at(*p), seq_at(p[0], p[1] + 1, p[2])) for p in SEQ])


def move_core(value):
    return lax.ppermute(value, "seq", [(seq_at(*p), seq_at(p[0], p[1], p[2] + 1)) for p in SEQ])


def move_x(value, step):
    return lax.ppermute(
        value, "dp", [(x * 4 + z, ((x + step) % 4) * 4 + z) for x, z in DP]
    )


def move_z_lo(value, step):
    return lax.ppermute(value, "dp", [(x * 4 + z, x * 4 + (z + step) % 4) for x, z in DP])


def halo(block):
    forward = [(i, i + 1) for i in range(15)]
    backward = [(i + 1, i) for i in range(15)]
    low = lax.ppermute(block[-HALF:], "seq", forward)
    high = lax.ppermute(block[:HALF], "seq", backward)
    return jnp.concatenate([low, block, high], axis=0)


def part(value, index, size, axis):
    return lax.dynamic_slice_in_dim(value, index * size, size, axis)


def reduce_out(hidden, cot_pair):
    bf16, f32 = jnp.bfloat16, jnp.float32
    seq = lax.axis_index("seq")
    y, z_hi, core = seq // 4, (seq // 2) % 2, seq % 2
    hidden_pair = jnp.concatenate([hidden, move_core(hidden)], axis=0)

    def chunk(step):
        rows = part(hidden_pair, (y + step) % 4, 384, 1)
        return lax.dot_general(
            rows, cot_pair, (((0,), (0,)), ((), ())), preferred_element_type=f32
        )

    far = chunk(2).astype(bf16)
    up_a = move_y(far[:, :384], 1)
    down_b = move_y(far[:, 384:], -1)
    above = chunk(1)
    below = chunk(3)
    up_b = move_y(above[:, 384:].astype(bf16), 1)
    down_a = move_y(below[:, :384].astype(bf16), -1)
    own = chunk(0)
    up_a = move_y((above[:, :384] + up_a.astype(f32)).astype(bf16), 1)
    down_b = move_y((below[:, 384:] + down_b.astype(f32)).astype(bf16), -1)
    low = own[:, :384] + down_a.astype(f32) + up_a.astype(f32)
    high = own[:, 384:] + up_b.astype(f32) + down_b.astype(f32)
    total = jnp.concatenate([low, high], axis=1)
    other = move_z_hi(part(total, 1 - z_hi, 192, 0).astype(bf16))
    total = part(total, z_hi, 192, 0) + other.astype(f32)
    square = total * total
    mine = part(square, core, 96, 0)
    other = move_core(part(square, 1 - core, 96, 0).astype(bf16)).astype(f32)
    square = jnp.concatenate(
        [jnp.where(core == 0, mine, other), jnp.where(core == 0, other, mine)], axis=1
    )
    dp = lax.axis_index("dp")
    x, z_lo = dp // 4, dp % 4
    received = [move_x(part(square, (x + k) % 4, 384, 1).astype(bf16), k) for k in (1, 2, 3)]
    square = part(square, x, 384, 1)
    for value in received:
        square = square + value.astype(f32)
    received = [move_z_lo(part(square, (z_lo + k) % 4, 96, 1).astype(bf16), k) for k in (1, 2, 3)]
    square = part(square, z_lo, 96, 1)
    for value in received:
        square = square + value.astype(f32)
    return square


def reduce_rows(kernel_grad, gain_gradient):
    rows = jnp.concatenate([kernel_grad, gain_gradient[None]], axis=0)
    rows = rows.reshape(KW + 1, 16, 96).transpose(1, 0, 2).reshape(16, (KW + 1) * 96)
    rows = lax.all_to_all(rows, "seq", 0, 0, tiled=True).sum(axis=0)
    square = (rows * rows).reshape(KW + 1, 96)
    kernel = square[:KW].reshape(16, 2 * 96)
    gain = jnp.broadcast_to(square[KW][None], (16, 96))
    rows = jnp.concatenate([kernel, gain], axis=1)
    rows = lax.all_to_all(rows, "dp", 0, 0, tiled=True).sum(axis=0)
    return rows[: 2 * 96].reshape(2, 96), rows[2 * 96 :]


def on_device(frames_in, cotangent, lengths, out_weight, conv_kernel, layer_norm_gain):
    bf16, f32 = jnp.bfloat16, jnp.float32
    frame_count = frames_in.shape[1]
    width = out_weight.shape[0]
    seq = lax.axis_index("seq")
    core = seq % 2
    position = seq * frame_count + jnp.arange(frame_count, dtype=jnp.int32)
    valid = (position < lengths[0])[:, None]
    masked = jnp.where(valid, frames_in[0], jnp.zeros((), bf16))
    padded_wide = halo(masked).astype(f32)
    grad_out = jnp.where(valid, cotangent[0], jnp.zeros((), bf16))
    cot_pair = jnp.concatenate(
        [part(grad_out, core, 768, 1), move_core(part(grad_out, 1 - core, 768, 1))], axis=0
    )
    conv_out = jnp.zeros((frame_count, width), f32)
    for offset in range(KW):
        conv_out = conv_out + conv_kernel[offset] * padded_wide[offset : offset + frame_count]
    row_mean = jnp.mean(conv_out, axis=1, keepdims=True)
    centered = conv_out - row_mean
    inverse_deviation = lax.rsqrt(jnp.mean(centered * centered, axis=1, keepdims=True) + 1e-05)
    standardized = centered * inverse_deviation
    normalized = standardized * layer_norm_gain
    sigma = jax.nn.sigmoid(normalized)
    hidden = (normalized * sigma).astype(bf16)
    fisher_out = reduce_out(hidden, cot_pair)
    hidden_grad = lax.dot_general(
        grad_out, out_weight, (((1,), (1,)), ((), ())), preferred_element_type=f32
    )
    normalized_grad = hidden_grad * (sigma + normalized * sigma * (1.0 - sigma))
    gain_gradient = jnp.sum(normalized_grad * standardized, axis=0)
    scaled = normalized_grad * layer_norm_gain
    conv_grad = inverse_deviation * (
        scaled
        - jnp.mean(scaled, axis=1, keepdims=True)
        - standardized * jnp.mean(scaled * standardized, axis=1, keepdims=True)
    )
    conv_grad = conv_grad.astype(bf16)
    conv_wide = conv_grad.astype(f32)
    kernel_grad = jnp.stack(
        [
            jnp.sum(conv_wide * padded_wide[offset : offset + frame_count], axis=0)
            for offset in range(KW)
        ]
    )
    fisher_kernel, fisher_gain = reduce_rows(kernel_grad, gain_gradient)
    grad_padded = halo(conv_grad).astype(f32)
    summed = jnp.zeros((frame_count, width), f32)
    for offset in range(KW):
        begin = KW - offset
        summed = summed + conv_kernel[offset] * grad_padded[begin : begin + frame_count]
    input_grad = jnp.where(valid, summed, 0.0).astype(bf16)[None]
    return input_grad, fisher_out / 16, fisher_kernel / 16, fisher_gain / 16


def solution(mesh):
    return jax.shard_map(
        on_device,
        mesh=mesh,
        in_specs=(P("dp", "seq", None), P("dp", "seq", None), P("dp"), P(), P(), P()),
        out_specs=(P("dp", "seq", None), P("seq", "dp"), P("dp", "seq"), P("seq")),
        check_vma=False,
    )
```

```python
import jax
import jax.numpy as jnp
from jax import lax
from jax.experimental import pallas as pl
from jax.experimental.pallas import tpu as pltpu
from jax.sharding import PartitionSpec as P

KW = 32
HALF = KW // 2
WIDTH = 1536
ROWS = 256
INNER = ROWS - 2 * HALF
LANES = 128
BF16, F32 = jnp.bfloat16, jnp.float32
SEQ = [(y, z, c) for y in range(4) for z in range(2) for c in range(2)]
DP = [(x, z) for x in range(4) for z in range(4)]
VMEM = pl.BlockSpec(memory_space=pltpu.VMEM)
SMEM = pl.BlockSpec(memory_space=pltpu.SMEM)


def seq_at(y, z, c):
    return ((y % 4) * 2 + z % 2) * 2 + c % 2


def move_y(value, step):
    return lax.ppermute(value, "seq", [(seq_at(*p), seq_at(p[0] + step, p[1], p[2])) for p in SEQ])


def move_z_hi(value):
    return lax.ppermute(value, "seq", [(seq_at(*p), seq_at(p[0], p[1] + 1, p[2])) for p in SEQ])


def move_core(value):
    return lax.ppermute(value, "seq", [(seq_at(*p), seq_at(p[0], p[1], p[2] + 1)) for p in SEQ])


def move_x(value, step):
    return lax.ppermute(value, "dp", [(x * 4 + z, ((x + step) % 4) * 4 + z) for x, z in DP])


def move_z_lo(value, step):
    return lax.ppermute(value, "dp", [(x * 4 + z, x * 4 + (z + step) % 4) for x, z in DP])


def halo(block):
    low = lax.ppermute(block[-HALF:], "seq", [(i, i + 1) for i in range(15)])
    high = lax.ppermute(block[:HALF], "seq", [(i + 1, i) for i in range(15)])
    return jnp.concatenate([low, high], axis=0)


def part(value, index, size, axis):
    return lax.dynamic_slice_in_dim(value, index * size, size, axis)


def masked_rows(rows, first, length):
    position = first + lax.broadcasted_iota(jnp.int32, rows.shape, 0)
    return jnp.where(position < length, rows.astype(F32), 0.0)


def depthwise(x_ref, taps_ref, out_ref, rows, chunk, finish=None, taps=None):
    taps = {j: j for j in range(KW)} if taps is None else taps

    def lane_block(i, carry):
        lanes = pl.ds(pl.multiple_of(i * LANES, LANES), LANES)
        for begin in range(0, rows, chunk):
            x = x_ref[pl.ds(begin, chunk + KW), lanes]
            total = None
            for shift in range(8):
                span = chunk if shift == 0 else chunk + 8
                sum_ = None
                for j in range(shift, KW + 1, 8):
                    if j in taps:
                        term = taps_ref[pl.ds(taps[j], 1), lanes] * x[j - shift : j - shift + span]
                        sum_ = term if sum_ is None else sum_ + term
                if shift:
                    sum_ = pltpu.roll(sum_, span - shift, 0)[:chunk]
                total = sum_ if total is None else total + sum_
            if finish is not None:
                total = finish(total, begin)
            out_ref[pl.ds(begin, chunk), lanes] = total
        return carry

    lax.fori_loop(0, WIDTH // LANES, lane_block, 0)


def normalise_rows(conv, upstream, gain, valid):
    mean = jnp.sum(conv, axis=1, keepdims=True) * (1.0 / WIDTH)
    centered = conv - mean
    variance = jnp.sum(centered * centered, axis=1, keepdims=True) * (1.0 / WIDTH)
    inverse = lax.rsqrt(variance + 1e-05)
    standardized = centered * inverse
    normalized = standardized * gain
    sigma = 1.0 / (1.0 + jnp.exp(-normalized))
    hidden = normalized * sigma
    grad = jnp.where(valid, upstream * (sigma + hidden * (1.0 - sigma)), 0.0)
    gain_term = grad * standardized
    scaled = grad * gain
    first = jnp.sum(scaled, axis=1, keepdims=True) * (1.0 / WIDTH)
    second = jnp.sum(scaled * standardized, axis=1, keepdims=True) * (1.0 / WIDTH)
    conv_grad = inverse * (scaled - first - standardized * second)
    return jnp.where(valid, hidden, 0.0), conv_grad, gain_term


def row_blocks(conv_ref, grad_ref, gain_ref, hidden_ref, conv_grad_ref, gain_sum, rows, offset, first, length):
    def block(i, total):
        local = pl.ds(pl.multiple_of(i * 16, 16), 16)
        whole = pl.ds(pl.multiple_of(i * 16 + offset, 16), 16)
        position = first + offset + i * 16 + lax.broadcasted_iota(jnp.int32, (16, 1), 0)
        hidden, conv_grad, gain_term = normalise_rows(
            conv_ref[local, :], grad_ref[whole, :], gain_ref[...], position < length
        )
        hidden_ref[whole, :] = hidden.astype(BF16)
        conv_grad_ref[whole, :] = conv_grad.astype(BF16)
        return total + gain_term[:8] + gain_term[8:]

    gain_sum[...] = lax.fori_loop(0, rows // 16, block, jnp.zeros((8, WIDTH), F32))


def inner_kernel(where, frames, upstream, taps, gain, hidden, conv_grad, gain_sum, x, conv):
    x[...] = masked_rows(frames[...], where[0], where[1])
    depthwise(x, taps, conv, INNER, 112)
    row_blocks(conv, upstream, gain, hidden, conv_grad, gain_sum, INNER, HALF, where[0], where[1])


def edge_kernel(where, frames, sides, upstream, taps, gain, _, __, hidden, conv_grad, gain_sum, x, conv):
    bottom = pl.program_id(0)
    first, length = where[0] + bottom * (ROWS - HALF), where[1]
    block = frames[...].astype(F32)
    side = sides[...].astype(F32)

    @pl.when(bottom == 0)
    def _top():
        x[pl.ds(0, HALF), :] = side
        x[pl.ds(HALF, 2 * HALF), :] = block

    @pl.when(bottom == 1)
    def _bottom():
        x[pl.ds(0, 2 * HALF), :] = block
        x[pl.ds(2 * HALF, HALF), :] = side

    x[...] = masked_rows(x[...], first - HALF, length)
    depthwise(x, taps, conv, HALF, HALF)
    row_blocks(conv, upstream, gain, hidden, conv_grad, gain_sum, HALF, 0, first, length)


def rows_of(shape, dtype):
    return jax.ShapeDtypeStruct(shape, dtype)


def forward_inner(where, frames, upstream, taps, gain):
    return pl.pallas_call(
        inner_kernel,
        out_shape=(rows_of((ROWS, WIDTH), BF16), rows_of((ROWS, WIDTH), BF16), rows_of((8, WIDTH), F32)),
        in_specs=[SMEM, VMEM, VMEM, VMEM, VMEM],
        out_specs=(VMEM, VMEM, VMEM),
        scratch_shapes=[pltpu.VMEM((ROWS, WIDTH), F32), pltpu.VMEM((INNER, WIDTH), F32)],
        compiler_params=pltpu.CompilerParams(vmem_limit_bytes=32 << 20),
        cost_estimate=pl.CostEstimate(flops=60_000_000, bytes_accessed=4_000_000, transcendentals=800_000),
        name="forward_inner",
    )(where, frames, upstream, taps, gain)


def forward_edge(where, frames, sides, upstream, taps, gain, hidden, conv_grad):
    return pl.pallas_call(
        edge_kernel,
        grid=(2,),
        out_shape=(rows_of((ROWS, WIDTH), BF16), rows_of((ROWS, WIDTH), BF16), rows_of((16, WIDTH), F32)),
        in_specs=[
            SMEM,
            pl.BlockSpec((2 * HALF, WIDTH), lambda i: (7 * i, 0)),
            pl.BlockSpec((HALF, WIDTH), lambda i: (i, 0)),
            pl.BlockSpec((HALF, WIDTH), lambda i: (15 * i, 0)),
            pl.BlockSpec((KW, WIDTH), lambda i: (0, 0)),
            pl.BlockSpec((1, WIDTH), lambda i: (0, 0)),
            pl.BlockSpec(memory_space=pl.ANY),
            pl.BlockSpec(memory_space=pl.ANY),
        ],
        out_specs=(
            pl.BlockSpec((HALF, WIDTH), lambda i: (15 * i, 0)),
            pl.BlockSpec((HALF, WIDTH), lambda i: (15 * i, 0)),
            pl.BlockSpec((8, WIDTH), lambda i: (i, 0)),
        ),
        scratch_shapes=[pltpu.VMEM((3 * HALF, WIDTH), F32), pltpu.VMEM((HALF, WIDTH), F32)],
        input_output_aliases={6: 0, 7: 1},
        compiler_params=pltpu.CompilerParams(vmem_limit_bytes=32 << 20),
        cost_estimate=pl.CostEstimate(flops=8_000_000, bytes_accessed=1_000_000, transcendentals=100_000),
        name="forward_edge",
    )(where, frames, sides, upstream, taps, gain, hidden, conv_grad)


def kernel_grad_kernel(where, frames, sides, conv_grad, gain_inner, gain_edge, out, x, g):
    first, length = where[0], where[1]
    x[pl.ds(0, HALF), :] = masked_rows(sides[pl.ds(0, HALF), :], first - HALF, length)
    x[pl.ds(HALF, ROWS), :] = masked_rows(frames[...], first, length)
    x[pl.ds(HALF + ROWS, HALF), :] = masked_rows(sides[pl.ds(HALF, HALF), :], first + ROWS, length)
    g[pl.ds(0, 8), :] = jnp.zeros((8, WIDTH), F32)
    g[pl.ds(8, ROWS), :] = conv_grad[...].astype(F32)
    g[pl.ds(8 + ROWS, 8), :] = jnp.zeros((8, WIDTH), F32)
    chunk = 88

    def lane_block(i, carry):
        lanes = pl.ds(pl.multiple_of(i * LANES, LANES), LANES)
        sums = [None] * KW
        for begin in range(0, ROWS + 8, chunk):
            rows = x_rows = x[pl.ds(begin, chunk + KW - 8), lanes]
            grad = g[pl.ds(begin, chunk + 8), lanes]
            for shift in range(8):
                moved = grad[8:] if shift == 0 else pltpu.roll(grad, shift, 0)[8:]
                for a in range(KW // 8):
                    j = 8 * a + shift
                    product = (moved * x_rows[8 * a : 8 * a + chunk]).reshape(chunk // 8, 8, LANES)
                    product = jnp.sum(product, axis=0)
                    sums[j] = product if sums[j] is None else sums[j] + product
        out[pl.ds(0, KW), lanes] = jnp.concatenate(
            [jnp.sum(value, axis=0, keepdims=True) for value in sums], axis=0
        )
        gain = gain_inner[:, lanes] + gain_edge[pl.ds(0, 8), lanes] + gain_edge[pl.ds(8, 8), lanes]
        out[pl.ds(KW, 8), lanes] = jnp.broadcast_to(jnp.sum(gain, axis=0, keepdims=True), (8, LANES))
        return carry

    lax.fori_loop(0, WIDTH // LANES, lane_block, 0)


def kernel_grads(where, frames, sides, conv_grad, gain_inner, gain_edge):
    return pl.pallas_call(
        kernel_grad_kernel,
        out_shape=rows_of((KW + 8, WIDTH), F32),
        in_specs=[SMEM, VMEM, VMEM, VMEM, VMEM, VMEM],
        out_specs=VMEM,
        scratch_shapes=[pltpu.VMEM((ROWS + KW, WIDTH), F32), pltpu.VMEM((ROWS + 16, WIDTH), F32)],
        compiler_params=pltpu.CompilerParams(vmem_limit_bytes=32 << 20),
        cost_estimate=pl.CostEstimate(flops=50_000_000, bytes_accessed=2_000_000, transcendentals=0),
        name="kernel_grads",
    )(where, frames, sides, conv_grad, gain_inner, gain_edge)


def input_grad_kernel(where, conv_grad, sides, taps, out, g):
    first, length = where[0], where[1]
    g[pl.ds(0, HALF), :] = sides[pl.ds(0, HALF), :].astype(F32)
    g[pl.ds(HALF, ROWS), :] = conv_grad[...].astype(F32)
    g[pl.ds(HALF + ROWS, HALF), :] = sides[pl.ds(HALF, HALF), :].astype(F32)

    def finish(total, begin):
        return masked_rows(total, first + begin, length).astype(BF16)

    depthwise(g, taps, out, ROWS, 64, finish, {j: KW - j for j in range(1, KW + 1)})


def input_grads(where, conv_grad, sides, taps):
    return pl.pallas_call(
        input_grad_kernel,
        out_shape=rows_of((ROWS, WIDTH), BF16),
        in_specs=[SMEM, VMEM, VMEM, VMEM],
        out_specs=VMEM,
        scratch_shapes=[pltpu.VMEM((ROWS + KW, WIDTH), F32)],
        compiler_params=pltpu.CompilerParams(vmem_limit_bytes=32 << 20),
        cost_estimate=pl.CostEstimate(flops=50_000_000, bytes_accessed=2_000_000, transcendentals=0),
        name="input_grads",
    )(where, conv_grad, sides, taps)


def reduce_out(hidden, cot_pair):
    seq = lax.axis_index("seq")
    y, z_hi, core = seq // 4, (seq // 2) % 2, seq % 2
    hidden_pair = jnp.concatenate([hidden, move_core(hidden)], axis=0)

    def chunk(step):
        rows = part(hidden_pair, (y + step) % 4, 384, 1)
        return lax.dot_general(
            rows, cot_pair, (((0,), (0,)), ((), ())), preferred_element_type=F32
        )

    far = chunk(2).astype(BF16)
    up_a = move_y(far[:, :384], 1)
    down_b = move_y(far[:, 384:], -1)
    above = chunk(1)
    below = chunk(3)
    up_b = move_y(above[:, 384:].astype(BF16), 1)
    down_a = move_y(below[:, :384].astype(BF16), -1)
    own = chunk(0)
    up_a = move_y((above[:, :384] + up_a.astype(F32)).astype(BF16), 1)
    down_b = move_y((below[:, 384:] + down_b.astype(F32)).astype(BF16), -1)
    low = own[:, :384] + down_a.astype(F32) + up_a.astype(F32)
    high = own[:, 384:] + up_b.astype(F32) + down_b.astype(F32)
    total = jnp.concatenate([low, high], axis=1)
    sent = total.astype(BF16)

    def rows_for(z, c):
        return part(sent, 2 * z + c, 96, 0)

    across = move_z_hi(rows_for(1 - z_hi, core))
    diagonal = lax.ppermute(
        rows_for(1 - z_hi, 1 - core), "seq", [(seq_at(*p), seq_at(p[0], p[1] + 1, p[2] + 1)) for p in SEQ]
    )
    beside = move_core(rows_for(z_hi, 1 - core))
    mine = part(total, 2 * z_hi + core, 96, 0) + across.astype(F32)
    other = beside.astype(F32) + diagonal.astype(F32)
    square = jnp.concatenate(
        [jnp.where(core == 0, mine, other), jnp.where(core == 0, other, mine)], axis=1
    )
    square = square * square
    dp = lax.axis_index("dp")
    x, z_lo = dp // 4, dp % 4
    received = [move_x(part(square, (x + k) % 4, 384, 1).astype(BF16), k) for k in (1, 2, 3)]
    square = part(square, x, 384, 1)
    for value in received:
        square = square + value.astype(F32)
    received = [move_z_lo(part(square, (z_lo + k) % 4, 96, 1).astype(BF16), k) for k in (1, 2, 3)]
    square = part(square, z_lo, 96, 1)
    for value in received:
        square = square + value.astype(F32)
    return square


def reduce_rows(rows):
    rows = rows[: KW + 1].reshape(KW + 1, 16, 96).transpose(1, 0, 2).reshape(16, (KW + 1) * 96)
    rows = lax.all_to_all(rows, "seq", 0, 0, tiled=True).sum(axis=0)
    square = (rows * rows).reshape(KW + 1, 96)
    kernel = square[:KW].reshape(16, 2 * 96)
    gain = jnp.broadcast_to(square[KW][None], (16, 96))
    rows = jnp.concatenate([kernel, gain], axis=1)
    rows = lax.all_to_all(rows, "dp", 0, 0, tiled=True).sum(axis=0)
    return rows[: 2 * 96].reshape(2, 96), rows[2 * 96 :]


def on_device(frames_in, cotangent, lengths, out_weight, conv_kernel, layer_norm_gain):
    seq = lax.axis_index("seq")
    core = seq % 2
    where = jnp.stack([seq * ROWS, lengths[0]]).astype(jnp.int32)
    frames, cot = frames_in[0], cotangent[0]
    gain = layer_norm_gain[None]
    sides = halo(frames)
    cot_pair = jnp.concatenate([part(cot, core, 768, 1), move_core(part(cot, 1 - core, 768, 1))], axis=0)
    upstream = lax.dot_general(cot, out_weight, (((1,), (1,)), ((), ())), preferred_element_type=F32)
    hidden, conv_grad, gain_inner = forward_inner(where, frames, upstream, conv_kernel, gain)
    hidden, conv_grad, gain_edge = forward_edge(
        where, frames, sides, upstream, conv_kernel, gain, hidden, conv_grad
    )
    fisher_out = reduce_out(hidden, cot_pair)
    grad_sides = halo(conv_grad)
    rows = kernel_grads(where, frames, sides, conv_grad, gain_inner, gain_edge)
    fisher_kernel, fisher_gain = reduce_rows(rows)
    input_grad = input_grads(where, conv_grad, grad_sides, conv_kernel)
    return input_grad[None], fisher_out / 16, fisher_kernel / 16, fisher_gain / 16


def solution(mesh):
    return jax.shard_map(
        on_device,
        mesh=mesh,
        in_specs=(P("dp", "seq", None), P("dp", "seq", None), P("dp"), P(), P(), P()),
        out_specs=(P("dp", "seq", None), P("seq", "dp"), P("dp", "seq"), P("seq")),
        check_vma=False,
    )
```

```python
import jax
import jax.numpy as jnp
from jax import lax
from jax.experimental import pallas as pl
from jax.experimental.pallas import tpu as pltpu
from jax.sharding import PartitionSpec as P

KW = 32
HALF = KW // 2
WIDTH = 1536
ROWS = 256
INNER = ROWS - 2 * HALF
LANES = 128
QUARTER = WIDTH // 4
BLOCK = WIDTH // 16
EXTRA = 16
BF16, F32 = jnp.bfloat16, jnp.float32
SEQ = [(y, z, c) for y in range(4) for z in range(2) for c in range(2)]
DP = [(x, z) for x in range(4) for z in range(4)]
VMEM = pl.BlockSpec(memory_space=pltpu.VMEM)
SMEM = pl.BlockSpec(memory_space=pltpu.SMEM)
ANY = pl.BlockSpec(memory_space=pl.ANY)
LIMIT = pltpu.CompilerParams(vmem_limit_bytes=32 << 20)


def seq_at(y, z, c):
    return ((y % 4) * 2 + z % 2) * 2 + c % 2


def move_y(value, step):
    return lax.ppermute(value, "seq", [(seq_at(*p), seq_at(p[0] + step, p[1], p[2])) for p in SEQ])


def move_z_hi(value):
    return lax.ppermute(value, "seq", [(seq_at(*p), seq_at(p[0], p[1] + 1, p[2])) for p in SEQ])


def move_core(value):
    return lax.ppermute(value, "seq", [(seq_at(*p), seq_at(p[0], p[1], p[2] + 1)) for p in SEQ])


def move_x(value, step):
    return lax.ppermute(value, "dp", [(x * 4 + z, ((x + step) % 4) * 4 + z) for x, z in DP])


def move_z_lo(value, step):
    return lax.ppermute(value, "dp", [(x * 4 + z, x * 4 + (z + step) % 4) for x, z in DP])


def move_neighbour(value):
    return lax.ppermute(value, "seq", [(i, (i + 1) % 16 if i % 2 else (i - 1) % 16) for i in range(16)])


def masked_rows(rows, first, length):
    position = first + lax.broadcasted_iota(jnp.int32, rows.shape, 0)
    return jnp.where((position >= 0) & (position < length), rows.astype(F32), 0.0)


def low_rows(core, chips, beside, begin, count):
    rows = pl.ds(begin, count)
    return jnp.where(core == 0, chips[rows, :].astype(F32), beside[rows, :].astype(F32))


def high_rows(core, chips, beside, begin, count):
    rows = pl.ds(begin, count)
    return jnp.where(core == 0, beside[rows, :].astype(F32), chips[rows, :].astype(F32))


def rows_of(shape, dtype):
    return jax.ShapeDtypeStruct(shape, dtype)


def rows_of(shape, dtype):
    return jax.ShapeDtypeStruct(shape, dtype)


def depthwise(x_ref, taps_ref, out_ref, rows, chunk, finish=None, taps=None, keep=None):
    taps = {j: j for j in range(KW)} if taps is None else taps

    def lane_block(i, carry):
        lanes = pl.ds(pl.multiple_of(i * LANES, LANES), LANES)
        for place, begin in enumerate(range(0, rows, chunk) if keep is None else keep):
            x = x_ref[pl.ds(begin, chunk + KW), lanes]
            total = None
            for shift in range(8):
                span = chunk if shift == 0 else chunk + 8
                sum_ = None
                for j in range(shift, KW + 1, 8):
                    if j in taps:
                        term = taps_ref[pl.ds(taps[j], 1), lanes] * x[j - shift : j - shift + span]
                        sum_ = term if sum_ is None else sum_ + term
                if shift:
                    sum_ = pltpu.roll(sum_, span - shift, 0)[:chunk]
                total = sum_ if total is None else total + sum_
            if finish is not None:
                total = finish(total, begin)
            out_ref[pl.ds(place * chunk, chunk), lanes] = total
        return carry

    lax.fori_loop(0, WIDTH // LANES, lane_block, 0)


LANE_BLOCKS = [pl.ds(i * LANES, LANES) for i in range(WIDTH // LANES)]


def row_sum(terms):
    total = None
    for term in terms:
        total = term if total is None else total + term
    return jnp.sum(total, axis=1, keepdims=True)


def standardise(conv, taps, refs, begin, size, offset, first, length):
    hidden, standard, inverse = refs
    rows, out = pl.ds(begin, size), pl.ds(offset, size)
    mean = row_sum(conv[rows, lanes] for lanes in LANE_BLOCKS) * (1.0 / WIDTH)
    variance = row_sum(jnp.square(conv[rows, lanes] - mean) for lanes in LANE_BLOCKS) * (1.0 / WIDTH)
    scale = lax.rsqrt(variance + 1e-05)
    valid = first + lax.broadcasted_iota(jnp.int32, (size, 1), 0) < length
    for lanes in LANE_BLOCKS:
        value = (conv[rows, lanes] - mean) * scale
        standard[out, lanes] = value
        if hidden is not None:
            normal = value * taps[pl.ds(KW, 1), lanes]
            value = normal * (0.5 + 0.5 * jnp.tanh(0.5 * normal))
            hidden[out, lanes] = jnp.where(valid, value, 0.0).astype(BF16)
    inverse[out, :] = jnp.broadcast_to(scale, (size, LANES))


def inner_kernel(where, frames, taps, hidden, standard, inverse, x, conv):
    first, length = where[0], where[1]
    x[...] = masked_rows(frames[...], first, length)
    depthwise(x, taps, conv, INNER, 112)
    for begin in range(0, INNER, 112):
        refs = (hidden, standard, inverse)
        standardise(conv, taps, refs, begin, 112, 2 * HALF + begin, first + HALF + begin, length)


def edge_kernel(where, top, bottom, chips, beside, taps, _, __, ___, hidden, standard, inverse, x, conv, h, s, i):
    first, length, core = where[0], where[1], where[2]
    end = first + ROWS

    @pl.when(pl.program_id(0) == 0)
    def _both():
        x[pl.ds(0, HALF), :] = masked_rows(low_rows(core, chips, beside, HALF, HALF), first - HALF, length)
        x[pl.ds(HALF, 2 * HALF), :] = masked_rows(top[...], first, length)
        x[pl.ds(3 * HALF, 2 * HALF), :] = masked_rows(bottom[...], end - 2 * HALF, length)
        x[pl.ds(5 * HALF, HALF), :] = masked_rows(high_rows(core, chips, beside, 0, HALF), end, length)
        depthwise(x, taps, conv, 4 * HALF, HALF, keep=(0, 3 * HALF))
        standardise(conv, taps, (h, s, i), 0, HALF, 0, first, length)
        standardise(conv, taps, (h, s, i), HALF, HALF, HALF, end - HALF, length)

    rows = pl.ds(pl.multiple_of(pl.program_id(0) * HALF, HALF), HALF)
    hidden[...] = h[rows, :]
    standard[...] = s[rows, :]
    inverse[...] = i[rows, :]


def outer_kernel(where, top, bottom, chips, beside, taps, _, __, standard, inverse, x, conv, s, i):
    first, length, core = where[0], where[1], where[2]
    end = first + ROWS

    @pl.when(pl.program_id(0) == 0)
    def _both():
        x[pl.ds(0, 2 * HALF), :] = masked_rows(low_rows(core, chips, beside, 0, 2 * HALF), first - 2 * HALF, length)
        x[pl.ds(2 * HALF, HALF), :] = masked_rows(top[...], first, length)
        x[pl.ds(3 * HALF, HALF), :] = masked_rows(bottom[...], end - HALF, length)
        x[pl.ds(4 * HALF, 2 * HALF), :] = masked_rows(high_rows(core, chips, beside, 0, 2 * HALF), end, length)
        depthwise(x, taps, conv, 4 * HALF, HALF, keep=(0, 3 * HALF))
        standardise(conv, taps, (None, s, i), 0, 2 * HALF, 0, first, length)

    rows = pl.ds(pl.multiple_of(pl.program_id(0) * HALF, HALF), HALF)
    standard[...] = s[rows, :]
    inverse[...] = i[rows, :]


SPAN = ROWS + 2 * HALF
FORWARD = (rows_of((SPAN, WIDTH), BF16), rows_of((SPAN, WIDTH), F32), rows_of((SPAN, LANES), F32))


def forward_inner(where, frames, taps):
    return pl.pallas_call(
        inner_kernel,
        out_shape=FORWARD,
        in_specs=[SMEM, VMEM, VMEM],
        out_specs=(VMEM, VMEM, VMEM),
        scratch_shapes=[pltpu.VMEM((ROWS, WIDTH), F32), pltpu.VMEM((INNER, WIDTH), F32)],
        compiler_params=LIMIT,
        cost_estimate=pl.CostEstimate(flops=60_000_000, bytes_accessed=4_000_000, transcendentals=800_000),
        name="forward_inner",
    )(where, frames, taps)


def fixed(shape, row=0):
    return pl.BlockSpec(shape, lambda i: (row, 0))


SIDE = fixed((3 * HALF, WIDTH))
SCRATCH = [pltpu.VMEM((6 * HALF, WIDTH), F32), pltpu.VMEM((2 * HALF, WIDTH), F32)]
KEPT = [pltpu.VMEM((2 * HALF, WIDTH), BF16), pltpu.VMEM((2 * HALF, WIDTH), F32), pltpu.VMEM((2 * HALF, LANES), F32)]


def forward_edge(where, frames, chips, beside, taps, forward):
    def ends(i):
        return (1 + 15 * i, 0)

    return pl.pallas_call(
        edge_kernel,
        grid=(2,),
        out_shape=FORWARD,
        in_specs=[
            SMEM,
            fixed((2 * HALF, WIDTH)),
            fixed((2 * HALF, WIDTH), 7),
            SIDE,
            SIDE,
            fixed((KW + 1, WIDTH)),
            ANY,
            ANY,
            ANY,
        ],
        out_specs=(
            pl.BlockSpec((HALF, WIDTH), ends),
            pl.BlockSpec((HALF, WIDTH), ends),
            pl.BlockSpec((HALF, LANES), ends),
        ),
        scratch_shapes=SCRATCH + KEPT,
        input_output_aliases={6: 0, 7: 1, 8: 2},
        compiler_params=LIMIT,
        cost_estimate=pl.CostEstimate(flops=8_000_000, bytes_accessed=1_000_000, transcendentals=100_000),
        name="forward_edge",
    )(where, frames, frames, chips, beside, taps, *forward)


def forward_outer(where, frames, chips, beside, taps, standard, inverse):
    def ends(i):
        return (17 * i, 0)

    return pl.pallas_call(
        outer_kernel,
        grid=(2,),
        out_shape=FORWARD[1:],
        in_specs=[
            SMEM,
            fixed((HALF, WIDTH)),
            fixed((HALF, WIDTH), 15),
            SIDE,
            SIDE,
            fixed((KW + 1, WIDTH)),
            ANY,
            ANY,
        ],
        out_specs=(pl.BlockSpec((HALF, WIDTH), ends), pl.BlockSpec((HALF, LANES), ends)),
        scratch_shapes=SCRATCH + KEPT[1:],
        input_output_aliases={6: 0, 7: 1},
        compiler_params=LIMIT,
        cost_estimate=pl.CostEstimate(flops=8_000_000, bytes_accessed=1_000_000, transcendentals=0),
        name="forward_outer",
    )(where, frames, frames, chips, beside, taps, standard, inverse)


def backward_rows(where, upstream, row, size, standard, inverse, taps, conv_grad, scaled):
    rows, held = pl.ds(row, size), pl.ds(0, size)
    position = where[0] - HALF + row + lax.broadcasted_iota(jnp.int32, (size, 1), 0)
    valid = (position >= 0) & (position < where[1])
    means, slopes, terms = None, None, []
    for lanes in LANE_BLOCKS:
        value = standard[rows, lanes]
        gain = taps[pl.ds(KW, 1), lanes]
        normal = value * gain
        sigma = 0.5 + 0.5 * jnp.tanh(0.5 * normal)
        grad = jnp.where(valid, upstream[rows, lanes] * (sigma + normal * sigma * (1.0 - sigma)), 0.0)
        terms.append(jnp.sum((grad * value).reshape(size // 8, 8, LANES), axis=0))
        grad = grad * gain
        scaled[held, lanes] = grad
        slope = grad * value
        means = grad if means is None else means + grad
        slopes = slope if slopes is None else slopes + slope
    mean = jnp.sum(means, axis=1, keepdims=True) * (1.0 / WIDTH)
    slope = jnp.sum(slopes, axis=1, keepdims=True) * (1.0 / WIDTH)
    scale = inverse[rows, :1]
    for lanes in LANE_BLOCKS:
        value = scaled[held, lanes] - mean - standard[rows, lanes] * slope
        conv_grad[rows, lanes] = (scale * value).astype(BF16)
    return terms


def backward_kernel(where, upstream, standard, inverse, taps, _, conv_grad, gain_sum, scaled):
    rest = (standard, inverse, taps, conv_grad, scaled)
    backward_rows(where, upstream, 0, HALF, *rest)
    backward_rows(where, upstream, HALF + ROWS, HALF, *rest)
    first = backward_rows(where, upstream, HALF, ROWS // 2, *rest)
    second = backward_rows(where, upstream, HALF + ROWS // 2, ROWS // 2, *rest)
    for lanes, one, two in zip(LANE_BLOCKS, first, second):
        gain_sum[:, lanes] = one + two


def backward(where, upstream, standard, inverse, taps, after):
    return pl.pallas_call(
        backward_kernel,
        out_shape=(rows_of((SPAN, WIDTH), BF16), rows_of((8, WIDTH), F32)),
        in_specs=[SMEM, VMEM, VMEM, VMEM, VMEM, ANY],
        out_specs=(VMEM, VMEM),
        scratch_shapes=[pltpu.VMEM((ROWS // 2, WIDTH), F32)],
        compiler_params=LIMIT,
        cost_estimate=pl.CostEstimate(flops=10_000_000, bytes_accessed=4_000_000, transcendentals=400_000),
        name="backward",
    )(where, upstream, standard, inverse, taps, after)


def kernel_grad_kernel(where, frames, chips, beside, conv_grad, gain_rows, _, keep, one, two, three, x, g, all_):
    first, length, core = where[0], where[1], where[2]
    x[pl.ds(0, HALF), :] = masked_rows(low_rows(core, chips, beside, HALF, HALF), first - HALF, length)
    x[pl.ds(HALF, ROWS), :] = masked_rows(frames[...], first, length)
    x[pl.ds(HALF + ROWS, HALF), :] = masked_rows(high_rows(core, chips, beside, 0, HALF), first + ROWS, length)
    g[pl.ds(0, 8), :] = jnp.zeros((8, WIDTH), F32)
    g[pl.ds(8, ROWS), :] = conv_grad[pl.ds(HALF, ROWS), :].astype(F32)
    g[pl.ds(8 + ROWS, 8), :] = jnp.zeros((8, WIDTH), F32)
    chunk = 88

    def lane_block(i, carry):
        lanes = pl.ds(pl.multiple_of(i * LANES, LANES), LANES)
        sums = [None] * KW
        for begin in range(0, ROWS + 8, chunk):
            x_rows = x[pl.ds(begin, chunk + KW - 8), lanes]
            grad = g[pl.ds(begin, chunk + 8), lanes]
            for shift in range(8):
                moved = grad[8:] if shift == 0 else pltpu.roll(grad, shift, 0)[8:]
                for a in range(KW // 8):
                    j = 8 * a + shift
                    product = (moved * x_rows[8 * a : 8 * a + chunk]).reshape(chunk // 8, 8, LANES)
                    product = jnp.sum(product, axis=0)
                    sums[j] = product if sums[j] is None else sums[j] + product
        all_[pl.ds(0, KW), lanes] = jnp.concatenate(
            [jnp.sum(value, axis=0, keepdims=True) for value in sums], axis=0
        )
        gain = jnp.sum(gain_rows[:, lanes], axis=0, keepdims=True)
        all_[pl.ds(KW, 8), lanes] = jnp.broadcast_to(gain, (8, LANES))
        return carry

    lax.fori_loop(0, WIDTH // LANES, lane_block, 0)
    for step, out in enumerate((keep, one, two, three)):
        out[...] = all_[:, pl.ds(pl.multiple_of(lax.rem(where[3] + step, 4) * QUARTER, QUARTER), QUARTER)]


def kernel_grads(where, frames, chips, beside, conv_grad, gain_rows, after):
    return pl.pallas_call(
        kernel_grad_kernel,
        out_shape=(rows_of((KW + 8, QUARTER), F32),) * 4,
        in_specs=[SMEM, VMEM, VMEM, VMEM, VMEM, VMEM, ANY],
        out_specs=(VMEM,) * 4,
        scratch_shapes=[
            pltpu.VMEM((ROWS + KW, WIDTH), F32),
            pltpu.VMEM((ROWS + 16, WIDTH), F32),
            pltpu.VMEM((KW + 8, WIDTH), F32),
        ],
        compiler_params=LIMIT,
        cost_estimate=pl.CostEstimate(flops=50_000_000, bytes_accessed=2_000_000, transcendentals=0),
        name="kernel_grads",
    )(where, frames, chips, beside, conv_grad, gain_rows, after)


def input_grad_kernel(where, conv_grad, taps, _, out, token, g):
    token[...] = jnp.zeros(token.shape, F32)
    first, length = where[0], where[1]
    g[...] = conv_grad[...].astype(F32)

    def finish(total, begin):
        return masked_rows(total, first + begin, length).astype(BF16)

    depthwise(g, taps, out, ROWS, 64, finish, {j: KW - j for j in range(1, KW + 1)})


def input_grads(where, conv_grad, taps, after):
    return pl.pallas_call(
        input_grad_kernel,
        out_shape=(rows_of((ROWS, WIDTH), BF16), rows_of((8, LANES), F32)),
        in_specs=[SMEM, VMEM, VMEM, ANY],
        out_specs=(VMEM, VMEM),
        scratch_shapes=[pltpu.VMEM((ROWS + KW, WIDTH), F32)],
        compiler_params=LIMIT,
        cost_estimate=pl.CostEstimate(flops=50_000_000, bytes_accessed=2_000_000, transcendentals=0),
        name="input_grads",
    )(where, conv_grad, taps, after)


def products_kernel(place, hidden, hidden_other, cot, cot_other, _, far_a, far_b, above_a, above_b, below_a, below_b, own):
    y, core = place[0], place[1]
    columns = pl.ds(pl.multiple_of(core * (WIDTH // 2), WIDTH // 2), WIDTH // 2)
    right, right_other = cot[:, columns], cot_other[:, columns]
    own_rows = pl.ds(HALF, ROWS)

    def chunk(step):
        rows = pl.ds(pl.multiple_of(lax.rem(y + step, 4) * QUARTER, QUARTER), QUARTER)
        dims = (((0,), (0,)), ((), ()))
        return lax.dot_general(
            hidden[own_rows, rows], right, dims, preferred_element_type=F32
        ) + lax.dot_general(hidden_other[own_rows, rows], right_other, dims, preferred_element_type=F32)

    for step, (a, b) in ((2, (far_a, far_b)), (1, (above_a, above_b)), (3, (below_a, below_b))):
        value = chunk(step)
        a[...] = value[:, :QUARTER].astype(a.dtype)
        b[...] = value[:, QUARTER:].astype(b.dtype)
    own[...] = chunk(0)


def products(place, hidden, hidden_other, cot, cot_other, after):
    half = (QUARTER, QUARTER)
    return pl.pallas_call(
        products_kernel,
        out_shape=(
            rows_of(half, BF16),
            rows_of(half, BF16),
            rows_of(half, F32),
            rows_of(half, BF16),
            rows_of(half, BF16),
            rows_of(half, F32),
            rows_of((QUARTER, 2 * QUARTER), F32),
        ),
        in_specs=[SMEM, VMEM, VMEM, VMEM, VMEM, ANY],
        out_specs=(VMEM,) * 7,
        compiler_params=LIMIT,
        cost_estimate=pl.CostEstimate(flops=1_200_000_000, bytes_accessed=8_000_000, transcendentals=0),
        name="products",
    )(place, hidden, hidden_other, cot, cot_other, after)


def seconds_kernel(above_a, up_a, below_b, down_b, _, second_a, second_b):
    second_a[...] = (above_a[...] + up_a[...].astype(F32)).astype(BF16)
    second_b[...] = (below_b[...] + down_b[...].astype(F32)).astype(BF16)


def seconds(above_a, up_a, below_b, down_b, after):
    return pl.pallas_call(
        seconds_kernel,
        out_shape=(rows_of((QUARTER, QUARTER), BF16),) * 2,
        in_specs=[VMEM, VMEM, VMEM, VMEM, ANY],
        out_specs=(VMEM,) * 2,
        compiler_params=LIMIT,
        cost_estimate=pl.CostEstimate(flops=300_000, bytes_accessed=2_400_000, transcendentals=0),
        name="seconds",
    )(above_a, up_a, below_b, down_b, after)


def blocks_kernel(
    place, own, down_a, up_a, up_b, down_b, k0, k1, k2, k3, mine, across, beside, diagonal, total, extra
):
    z_hi, core = place[2], place[1]
    total[:, :QUARTER] = own[:, :QUARTER] + (down_a[...].astype(F32) + up_a[...].astype(F32))
    total[:, QUARTER:] = own[:, QUARTER:] + (down_b[...].astype(F32) + up_b[...].astype(F32))
    sums = k0[...] + k1[...] + k2[...] + k3[...]
    extra[...] = jnp.zeros(extra.shape, F32)
    for block in range(4):
        for q in range(5):
            extra[block, pl.ds(0, 8), pl.ds(q * BLOCK, BLOCK)] = sums[
                8 * q : 8 * q + 8, block * BLOCK : (block + 1) * BLOCK
            ]
    for out, z, c in (
        (mine, z_hi, core),
        (across, 1 - z_hi, core),
        (beside, z_hi, 1 - core),
        (diagonal, 1 - z_hi, 1 - core),
    ):
        block = 2 * z + c
        out[pl.ds(0, BLOCK), :] = total[pl.ds(pl.multiple_of(block * BLOCK, BLOCK), BLOCK), :].astype(out.dtype)
        out[pl.ds(BLOCK, EXTRA), :] = extra[block].astype(out.dtype)


def blocks(place, own, down_a, up_a, up_b, down_b, rows):
    shape = (BLOCK + EXTRA, WIDTH // 2)
    return pl.pallas_call(
        blocks_kernel,
        out_shape=(rows_of(shape, F32),) + (rows_of(shape, BF16),) * 3,
        in_specs=[SMEM] + [VMEM] * 9,
        out_specs=(VMEM,) * 4,
        scratch_shapes=[pltpu.VMEM((QUARTER, 2 * QUARTER), F32), pltpu.VMEM((4, EXTRA, WIDTH // 2), F32)],
        compiler_params=LIMIT,
        cost_estimate=pl.CostEstimate(flops=1_000_000, bytes_accessed=4_000_000, transcendentals=0),
        name="blocks",
    )(place, own, down_a, up_a, up_b, down_b, *rows)


def squares_kernel(place, mine, across, beside, diagonal, _, keep, one, two, three, square, extra):
    core, x = place[1], place[3]
    half = WIDTH // 2
    rows, more = pl.ds(0, BLOCK), pl.ds(BLOCK, EXTRA)
    first = mine[rows, :] + across[rows, :].astype(F32)
    second = beside[rows, :].astype(F32) + diagonal[rows, :].astype(F32)
    square[rows, pl.ds(pl.multiple_of(core * half, half), half)] = first * first
    square[rows, pl.ds(pl.multiple_of((1 - core) * half, half), half)] = second * second
    sums = mine[more, :] + across[more, :].astype(F32) + beside[more, :].astype(F32) + diagonal[more, :].astype(F32)
    extra[...] = sums * sums
    square[more, :] = jnp.zeros((EXTRA, WIDTH), F32)
    for dp in range(16):
        columns = pl.ds(dp * BLOCK, BLOCK)
        square[pl.ds(BLOCK, 2), columns] = extra[pl.ds(2 * (dp % 4), 2), pl.ds(dp // 4 * BLOCK, BLOCK)]
        square[pl.ds(BLOCK + 2, 1), columns] = extra[pl.ds(0, 1), pl.ds(4 * BLOCK, BLOCK)]
    for step, out in enumerate((keep, one, two, three)):
        columns = pl.ds(pl.multiple_of(lax.rem(x + step, 4) * QUARTER, QUARTER), QUARTER)
        out[...] = square[:, columns].astype(out.dtype)


def squares(place, mine, across, beside, diagonal, after):
    shape = (BLOCK + EXTRA, QUARTER)
    return pl.pallas_call(
        squares_kernel,
        out_shape=(rows_of(shape, F32),) + (rows_of(shape, BF16),) * 3,
        in_specs=[SMEM] + [VMEM] * 4 + [ANY],
        out_specs=(VMEM,) * 4,
        scratch_shapes=[pltpu.VMEM((BLOCK + EXTRA, WIDTH), F32), pltpu.VMEM((EXTRA, WIDTH // 2), F32)],
        compiler_params=LIMIT,
        cost_estimate=pl.CostEstimate(flops=1_000_000, bytes_accessed=2_000_000, transcendentals=0),
        name="squares",
    )(place, mine, across, beside, diagonal, after)


def quarters_kernel(place, keep, one, two, three, own, out_one, out_two, out_three, parts):
    z_lo = place[4]
    total = keep[...] + one[...].astype(F32) + two[...].astype(F32) + three[...].astype(F32)
    for z in range(4):
        parts[lax.rem(z - z_lo + 4, 4)] = total[:, z * BLOCK : (z + 1) * BLOCK]
    for step, out in enumerate((own, out_one, out_two, out_three)):
        out[...] = parts[step].astype(out.dtype)


def quarters(place, keep, one, two, three):
    shape = (BLOCK + EXTRA, BLOCK)
    return pl.pallas_call(
        quarters_kernel,
        out_shape=(rows_of(shape, F32),) + (rows_of(shape, BF16),) * 3,
        in_specs=[SMEM] + [VMEM] * 4,
        out_specs=(VMEM,) * 4,
        scratch_shapes=[pltpu.VMEM((4,) + shape, F32)],
        compiler_params=LIMIT,
        cost_estimate=pl.CostEstimate(flops=1_000_000, bytes_accessed=1_000_000, transcendentals=0),
        name="quarters",
    )(place, keep, one, two, three)


def means_kernel(own, one, two, three, out, kernel, gain):
    total = own[...] + one[...].astype(F32) + two[...].astype(F32) + three[...].astype(F32)
    total = total * (1.0 / 16)
    out[...] = total[:BLOCK]
    kernel[...] = total[BLOCK : BLOCK + 2]
    gain[...] = total[BLOCK + 2 : BLOCK + 3]


def means(own, one, two, three):
    return pl.pallas_call(
        means_kernel,
        out_shape=(rows_of((BLOCK, BLOCK), F32), rows_of((2, BLOCK), F32), rows_of((1, BLOCK), F32)),
        in_specs=[VMEM] * 4,
        out_specs=(VMEM,) * 3,
        compiler_params=LIMIT,
        cost_estimate=pl.CostEstimate(flops=100_000, bytes_accessed=200_000, transcendentals=0),
        name="means",
    )(own, one, two, three)


def on_device(frames_in, cotangent, lengths, out_weight, conv_kernel, layer_norm_gain):
    seq, dp = lax.axis_index("seq"), lax.axis_index("dp")
    core = seq % 2
    where = jnp.stack([seq * ROWS, lengths[0], core, seq // 4]).astype(jnp.int32)
    place = jnp.stack([seq // 4, core, (seq // 2) % 2, dp // 4, dp % 4]).astype(jnp.int32)
    frames, cot = frames_in[0], cotangent[0]
    taps = jnp.concatenate([conv_kernel, layer_norm_gain[None]], axis=0)
    begin = jnp.concatenate([frames[: 2 * HALF], cot[:HALF]], axis=0)
    end = jnp.concatenate([frames[-2 * HALF :], cot[-HALF:]], axis=0)
    chips = move_neighbour(jnp.where(core == 0, begin, end))
    beside = move_core(jnp.where(core == 0, end, begin))
    cot_other = move_core(cot)
    forward = forward_inner(where, frames, taps)
    hidden, standard, inverse = forward_edge(where, frames, chips, beside, taps, forward)
    hidden_other = move_core(hidden)
    standard, inverse = forward_outer(where, frames, chips, beside, taps, standard, inverse)
    low = jnp.where(core == 0, chips[2 * HALF :], beside[2 * HALF :])
    high = jnp.where(core == 0, beside[2 * HALF :], chips[2 * HALF :])
    late_cot, _ = lax.optimization_barrier((jnp.concatenate([low, cot, high], axis=0), hidden))
    upstream = lax.dot_general(late_cot, out_weight, (((1,), (1,)), ((), ())), preferred_element_type=F32)
    far_a, far_b, above_a, above_b, below_a, below_b, own = products(
        place, hidden, hidden_other, cot, cot_other, upstream
    )
    up_a = move_y(far_a, 1)
    down_b = move_y(far_b, -1)
    up_b = move_y(above_b, 1)
    down_a = move_y(below_a, -1)
    conv_grad, gain_rows = backward(where, upstream, standard, inverse, taps, far_a)
    second_a, second_b = seconds(above_a, up_a, below_b, down_b, conv_grad)
    up_a = move_y(second_a, 1)
    down_b = move_y(second_b, -1)
    rows = kernel_grads(where, frames, chips, beside, conv_grad, gain_rows, second_a)
    rows = [rows[0]] + [move_y(rows[k], k) for k in (1, 2, 3)]
    mine, across, side, diagonal = blocks(place, own, down_a, up_a, up_b, down_b, rows)
    input_grad, token = input_grads(where, conv_grad, taps, across)
    across = move_z_hi(across)
    diagonal = lax.ppermute(
        diagonal, "seq", [(seq_at(*p), seq_at(p[0], p[1] + 1, p[2] + 1)) for p in SEQ]
    )
    side = move_core(side)
    keep, *sent = squares(place, mine, across, side, diagonal, token)
    keep, *sent = quarters(place, keep, *(move_x(value, k + 1) for k, value in enumerate(sent)))
    out, kernel, gain = means(keep, *(move_z_lo(value, k + 1) for k, value in enumerate(sent)))
    return input_grad[None], out, kernel, gain[0]


def solution(mesh):
    return jax.shard_map(
        on_device,
        mesh=mesh,
        in_specs=(P("dp", "seq", None), P("dp", "seq", None), P("dp"), P(), P(), P()),
        out_specs=(P("dp", "seq", None), P("seq", "dp"), P("dp", "seq"), P("seq")),
        check_vma=False,
    )
```

```python
import jax
import jax.numpy as jnp
from jax import lax
from jax.experimental import pallas as pl
from jax.experimental.pallas import tpu as pltpu
from jax.sharding import PartitionSpec as P

KW = 32
HALF = KW // 2
WIDTH = 1536
ROWS = 256
INNER = ROWS - 2 * HALF
LANES = 128
QUARTER = WIDTH // 4
BLOCK = WIDTH // 16
EXTRA = 16
MORE = 48
BF16, F32 = jnp.bfloat16, jnp.float32
SEQ = [(y, z, c) for y in range(4) for z in range(2) for c in range(2)]
DP = [(x, z) for x in range(4) for z in range(4)]
VMEM = pl.BlockSpec(memory_space=pltpu.VMEM)
SMEM = pl.BlockSpec(memory_space=pltpu.SMEM)
ANY = pl.BlockSpec(memory_space=pl.ANY)
LIMIT = pltpu.CompilerParams(vmem_limit_bytes=32 << 20)


def seq_at(y, z, c):
    return ((y % 4) * 2 + z % 2) * 2 + c % 2


def move_y(value, step):
    return lax.ppermute(value, "seq", [(seq_at(*p), seq_at(p[0] + step, p[1], p[2])) for p in SEQ])


def move_z_hi(value):
    return lax.ppermute(value, "seq", [(seq_at(*p), seq_at(p[0], p[1] + 1, p[2])) for p in SEQ])


def move_core(value):
    return lax.ppermute(value, "seq", [(seq_at(*p), seq_at(p[0], p[1], p[2] + 1)) for p in SEQ])


def move_x(value, step):
    return lax.ppermute(value, "dp", [(x * 4 + z, ((x + step) % 4) * 4 + z) for x, z in DP])


def move_z_lo(value, step):
    return lax.ppermute(value, "dp", [(x * 4 + z, x * 4 + (z + step) % 4) for x, z in DP])


def move_neighbour(value):
    return lax.ppermute(value, "seq", [(i, (i + 1) % 16 if i % 2 else (i - 1) % 16) for i in range(16)])


def place_of():
    seq, dp = lax.axis_index("seq"), lax.axis_index("dp")
    return seq >> 2, seq & 1, (seq >> 1) & 1, dp >> 2, dp & 3


def where_of(lengths):
    seq = lax.axis_index("seq")
    return seq * ROWS, lengths[0], seq & 1, seq >> 2


def masked_rows(rows, first, length):
    position = first + lax.broadcasted_iota(jnp.int32, rows.shape, 0)
    return jnp.where((position >= 0) & (position < length), rows.astype(F32), 0.0)


ALL = pl.ds(0, WIDTH)


def low_rows(core, chips, beside, begin, count, lanes=ALL):
    rows = pl.ds(begin, count)
    return jnp.where(core == 0, chips[rows, lanes].astype(F32), beside[rows, lanes].astype(F32))


def high_rows(core, chips, beside, begin, count, lanes=ALL):
    rows = pl.ds(begin, count)
    return jnp.where(core == 0, beside[rows, lanes].astype(F32), chips[rows, lanes].astype(F32))


def rows_of(shape, dtype):
    return jax.ShapeDtypeStruct(shape, dtype)


def rows_of(shape, dtype):
    return jax.ShapeDtypeStruct(shape, dtype)


def depthwise(x_ref, taps_ref, out_ref, rows, chunk, finish=None, taps=None, keep=None):
    taps = {j: j for j in range(KW)} if taps is None else taps

    def lane_block(i, carry):
        lanes = pl.ds(pl.multiple_of(i * LANES, LANES), LANES)
        for place, begin in enumerate(range(0, rows, chunk) if keep is None else keep):
            x = x_ref[pl.ds(begin, chunk + KW), lanes]
            total = None
            for shift in range(8):
                span = chunk if shift == 0 else chunk + 8
                sum_ = None
                for j in range(shift, KW + 1, 8):
                    if j in taps:
                        term = taps_ref[pl.ds(taps[j], 1), lanes] * x[j - shift : j - shift + span]
                        sum_ = term if sum_ is None else sum_ + term
                if shift:
                    sum_ = pltpu.roll(sum_, span - shift, 0)[:chunk]
                total = sum_ if total is None else total + sum_
            if finish is not None:
                total = finish(total, begin)
            out_ref[pl.ds(place * chunk, chunk), lanes] = total
        return carry

    lax.fori_loop(0, WIDTH // LANES, lane_block, 0)


LANE_BLOCKS = [pl.ds(i * LANES, LANES) for i in range(WIDTH // LANES)]


def row_sum(terms):
    total = None
    for term in terms:
        total = term if total is None else total + term
    return jnp.sum(total, axis=1, keepdims=True)


def standardise(conv, taps, refs, begin, size, offset, first, length):
    hidden, standard, inverse = refs
    rows, out = pl.ds(begin, size), pl.ds(offset, size)
    mean = row_sum(conv[rows, lanes] for lanes in LANE_BLOCKS) * (1.0 / WIDTH)
    variance = row_sum(jnp.square(conv[rows, lanes] - mean) for lanes in LANE_BLOCKS) * (1.0 / WIDTH)
    scale = lax.rsqrt(variance + 1e-05)
    valid = first + lax.broadcasted_iota(jnp.int32, (size, 1), 0) < length
    for lanes in LANE_BLOCKS:
        value = (conv[rows, lanes] - mean) * scale
        standard[out, lanes] = value
        if hidden is not None:
            normal = value * taps[pl.ds(KW, 1), lanes]
            value = normal * (0.5 + 0.5 * jnp.tanh(0.5 * normal))
            hidden[out, lanes] = jnp.where(valid, value, 0.0).astype(BF16)
    inverse[out, :] = jnp.broadcast_to(scale, (size, LANES))


def inner_kernel(lengths, frames, taps, hidden, standard, inverse, x, conv):
    where = where_of(lengths)
    first, length = where[0], where[1]
    x[...] = masked_rows(frames[...], first, length)
    depthwise(x, taps, conv, INNER, 112)
    for begin in range(0, INNER, 112):
        refs = (hidden, standard, inverse)
        standardise(conv, taps, refs, begin, 112, 2 * HALF + begin, first + HALF + begin, length)


def edge_kernel(lengths, top, bottom, chips, beside, taps, _, __, ___, hidden, standard, inverse, x, conv, h, s, i):
    where = where_of(lengths)
    first, length, core = where[0], where[1], where[2]
    end = first + ROWS

    @pl.when(pl.program_id(0) == 0)
    def _both():
        x[pl.ds(0, HALF), :] = masked_rows(low_rows(core, chips, beside, HALF, HALF), first - HALF, length)
        x[pl.ds(HALF, 2 * HALF), :] = masked_rows(top[...], first, length)
        x[pl.ds(3 * HALF, 2 * HALF), :] = masked_rows(bottom[...], end - 2 * HALF, length)
        x[pl.ds(5 * HALF, HALF), :] = masked_rows(high_rows(core, chips, beside, 0, HALF), end, length)
        depthwise(x, taps, conv, 4 * HALF, HALF, keep=(0, 3 * HALF))
        standardise(conv, taps, (h, s, i), 0, HALF, 0, first, length)
        standardise(conv, taps, (h, s, i), HALF, HALF, HALF, end - HALF, length)

    rows = pl.ds(pl.multiple_of(pl.program_id(0) * HALF, HALF), HALF)
    hidden[...] = h[rows, :]
    standard[...] = s[rows, :]
    inverse[...] = i[rows, :]


SPAN = ROWS + 2 * HALF
FORWARD = (rows_of((SPAN, WIDTH), BF16), rows_of((SPAN, WIDTH), F32), rows_of((SPAN, LANES), F32))


def forward_inner(lengths, frames, taps):
    return pl.pallas_call(
        inner_kernel,
        out_shape=FORWARD,
        in_specs=[SMEM, VMEM, VMEM],
        out_specs=(VMEM, VMEM, VMEM),
        scratch_shapes=[pltpu.VMEM((ROWS, WIDTH), F32), pltpu.VMEM((INNER, WIDTH), F32)],
        compiler_params=LIMIT,
        cost_estimate=pl.CostEstimate(flops=60_000_000, bytes_accessed=4_000_000, transcendentals=800_000),
        name="forward_inner",
    )(lengths, frames, taps)


def fixed(shape, row=0):
    return pl.BlockSpec(shape, lambda i: (row, 0))


SIDE = fixed((3 * HALF, WIDTH))
SCRATCH = [pltpu.VMEM((6 * HALF, WIDTH), F32), pltpu.VMEM((2 * HALF, WIDTH), F32)]
KEPT = [pltpu.VMEM((2 * HALF, WIDTH), BF16), pltpu.VMEM((2 * HALF, WIDTH), F32), pltpu.VMEM((2 * HALF, LANES), F32)]


def forward_edge(lengths, frames, chips, beside, taps, forward):
    def ends(i):
        return (1 + 15 * i, 0)

    return pl.pallas_call(
        edge_kernel,
        grid=(2,),
        out_shape=FORWARD,
        in_specs=[
            SMEM,
            fixed((2 * HALF, WIDTH)),
            fixed((2 * HALF, WIDTH), 7),
            SIDE,
            SIDE,
            fixed((KW + 1, WIDTH)),
            ANY,
            ANY,
            ANY,
        ],
        out_specs=(
            pl.BlockSpec((HALF, WIDTH), ends),
            pl.BlockSpec((HALF, WIDTH), ends),
            pl.BlockSpec((HALF, LANES), ends),
        ),
        scratch_shapes=SCRATCH + KEPT,
        input_output_aliases={6: 0, 7: 1, 8: 2},
        compiler_params=LIMIT,
        cost_estimate=pl.CostEstimate(flops=8_000_000, bytes_accessed=1_000_000, transcendentals=100_000),
        name="forward_edge",
    )(lengths, frames, frames, chips, beside, taps, *forward)


def backward_rows(first, length, upstream, begin, standard, row, inverse, taps, conv_grad, out_row, size, scaled):
    source, rows, held, out = pl.ds(begin, size), pl.ds(row, size), pl.ds(0, size), pl.ds(out_row, size)
    position = first + lax.broadcasted_iota(jnp.int32, (size, 1), 0)
    valid = (position >= 0) & (position < length)
    means, slopes, terms = None, None, []
    for lanes in LANE_BLOCKS:
        value = standard[rows, lanes]
        gain = taps[pl.ds(KW, 1), lanes]
        normal = value * gain
        sigma = 0.5 + 0.5 * jnp.tanh(0.5 * normal)
        grad = jnp.where(valid, upstream[source, lanes] * (sigma + normal * sigma * (1.0 - sigma)), 0.0)
        terms.append(jnp.sum((grad * value).reshape(size // 8, 8, LANES), axis=0))
        grad = grad * gain
        scaled[held, lanes] = grad
        slope = grad * value
        means = grad if means is None else means + grad
        slopes = slope if slopes is None else slopes + slope
    mean = jnp.sum(means, axis=1, keepdims=True) * (1.0 / WIDTH)
    slope = jnp.sum(slopes, axis=1, keepdims=True) * (1.0 / WIDTH)
    scale = inverse[rows, :1]
    for lanes in LANE_BLOCKS:
        value = scaled[held, lanes] - mean - standard[rows, lanes] * slope
        conv_grad[out, lanes] = (scale * value).astype(BF16)
    return terms


def backward_kernel(lengths, upstream, standard, inverse, taps, _, conv_grad, gain_sum, scaled):
    where = where_of(lengths)
    terms = []
    for begin in (0, ROWS // 2):
        span = HALF + begin
        refs = (upstream, span, standard, span, inverse, taps, conv_grad, begin, ROWS // 2, scaled)
        terms.append(backward_rows(where[0] + begin, where[1], *refs))
    for lanes, one, two in zip(LANE_BLOCKS, *terms):
        gain_sum[:, lanes] = one + two


def backward(lengths, upstream, standard, inverse, taps, after):
    return pl.pallas_call(
        backward_kernel,
        out_shape=(rows_of((ROWS, WIDTH), BF16), rows_of((8, WIDTH), F32)),
        in_specs=[SMEM, VMEM, VMEM, VMEM, VMEM, ANY],
        out_specs=(VMEM, VMEM),
        scratch_shapes=[pltpu.VMEM((ROWS // 2, WIDTH), F32)],
        compiler_params=LIMIT,
        cost_estimate=pl.CostEstimate(flops=10_000_000, bytes_accessed=4_000_000, transcendentals=400_000),
        name="backward",
    )(lengths, upstream, standard, inverse, taps, after)


def outer_kernel(lengths, frames, chips, beside, taps, upstream, _, out, x, conv, standard, inverse, scaled):
    where = where_of(lengths)
    first, length, core = where[0], where[1], where[2]
    end = first + ROWS
    top, bottom = frames[pl.ds(0, HALF), :], frames[pl.ds(ROWS - HALF, HALF), :]
    x[pl.ds(0, 2 * HALF), :] = masked_rows(low_rows(core, chips, beside, 0, 2 * HALF), first - 2 * HALF, length)
    x[pl.ds(2 * HALF, HALF), :] = masked_rows(top, first, length)
    x[pl.ds(3 * HALF, HALF), :] = masked_rows(bottom, end - HALF, length)
    x[pl.ds(4 * HALF, 2 * HALF), :] = masked_rows(high_rows(core, chips, beside, 0, 2 * HALF), end, length)
    depthwise(x, taps, conv, 4 * HALF, HALF, keep=(0, 3 * HALF))
    standardise(conv, taps, (None, standard, inverse), 0, 2 * HALF, 0, first, length)
    for row, begin, position in ((0, 0, first - HALF), (HALF, HALF + ROWS, end)):
        refs = (upstream, begin, standard, row, inverse, taps, out, row, HALF, scaled)
        backward_rows(position, length, *refs)


def outer_grads(lengths, frames, chips, beside, taps, upstream, after):
    return pl.pallas_call(
        outer_kernel,
        out_shape=rows_of((2 * HALF, WIDTH), BF16),
        in_specs=[SMEM] + [VMEM] * 5 + [ANY],
        out_specs=VMEM,
        scratch_shapes=SCRATCH + KEPT[1:] + [pltpu.VMEM((HALF, WIDTH), F32)],
        compiler_params=LIMIT,
        cost_estimate=pl.CostEstimate(flops=8_000_000, bytes_accessed=1_000_000, transcendentals=0),
        name="outer_grads",
    )(lengths, frames, chips, beside, taps, upstream, after)


SIDE_LANES = WIDTH // 2


def fill_rows(where, frames, chips, beside, conv_grad, x, g, columns):
    first, length, core = where[0], where[1], where[2]
    low = low_rows(core, chips, beside, HALF, HALF, columns)
    high = high_rows(core, chips, beside, 0, HALF, columns)
    x[pl.ds(0, HALF), :] = masked_rows(low, first - HALF, length)
    x[pl.ds(HALF, ROWS), :] = masked_rows(frames[:, columns], first, length)
    x[pl.ds(HALF + ROWS, HALF), :] = masked_rows(high, first + ROWS, length)
    g[pl.ds(0, 8), :] = jnp.zeros((8, SIDE_LANES), F32)
    g[pl.ds(8, ROWS), :] = conv_grad[:, columns].astype(F32)
    g[pl.ds(8 + ROWS, 8), :] = jnp.zeros((8, SIDE_LANES), F32)


def kernel_grad_lanes(x, g, gain_rows, out, offset):
    chunk = 88

    def lane_block(i, carry):
        lanes = pl.ds(pl.multiple_of(i * LANES, LANES), LANES)
        whole = pl.ds(pl.multiple_of(i * LANES + offset, LANES), LANES)
        sums = [None] * KW
        for begin in range(0, ROWS + 8, chunk):
            x_rows = x[pl.ds(begin, chunk + KW - 8), lanes]
            grad = g[pl.ds(begin, chunk + 8), lanes]
            for shift in range(8):
                moved = grad[8:] if shift == 0 else pltpu.roll(grad, shift, 0)[8:]
                for a in range(KW // 8):
                    j = 8 * a + shift
                    product = (moved * x_rows[8 * a : 8 * a + chunk]).reshape(chunk // 8, 8, LANES)
                    product = jnp.sum(product, axis=0)
                    sums[j] = product if sums[j] is None else sums[j] + product
        out[pl.ds(0, KW), whole] = jnp.concatenate(
            [jnp.sum(value, axis=0, keepdims=True) for value in sums], axis=0
        )
        gain = jnp.sum(gain_rows[:, whole], axis=0, keepdims=True)
        out[pl.ds(KW, 8), whole] = jnp.broadcast_to(gain, (8, LANES))
        return carry

    lax.fori_loop(0, SIDE_LANES // LANES, lane_block, 0)


def first_grad_kernel(lengths, frames, chips, beside, conv_grad, gain_rows, out, x, g):
    where = where_of(lengths)
    fill_rows(where, frames, chips, beside, conv_grad, x, g, pl.ds(0, SIDE_LANES))
    kernel_grad_lanes(x, g, gain_rows, out, 0)


def other_grad_kernel(lengths, frames, chips, beside, conv_grad, gain_rows, first, _, keep, one, two, three, x, g, rows):
    where = where_of(lengths)
    fill_rows(where, frames, chips, beside, conv_grad, x, g, pl.ds(SIDE_LANES, SIDE_LANES))
    rows[pl.ds(0, KW + 8), pl.ds(0, SIDE_LANES)] = first[...]
    kernel_grad_lanes(x, g, gain_rows, rows, SIDE_LANES)
    rows[pl.ds(KW + 8, 8), :] = jnp.zeros((8, WIDTH), F32)
    for step, out in enumerate((keep, one, two, three)):
        columns = pl.ds(pl.multiple_of(lax.rem(where[3] + step, 4) * QUARTER, QUARTER), QUARTER)
        out[...] = rows[:, columns].astype(out.dtype)


GRAD_SCRATCH = [pltpu.VMEM((ROWS + KW, SIDE_LANES), F32), pltpu.VMEM((ROWS + 16, SIDE_LANES), F32)]
GRAD_COST = pl.CostEstimate(flops=25_000_000, bytes_accessed=1_000_000, transcendentals=0)


def kernel_grads_first(lengths, frames, chips, beside, conv_grad, gain_rows):
    return pl.pallas_call(
        first_grad_kernel,
        out_shape=rows_of((KW + 8, SIDE_LANES), F32),
        in_specs=[SMEM] + [VMEM] * 5,
        out_specs=VMEM,
        scratch_shapes=GRAD_SCRATCH,
        compiler_params=LIMIT,
        cost_estimate=GRAD_COST,
        name="kernel_grads_first",
    )(lengths, frames, chips, beside, conv_grad, gain_rows)


def kernel_grads_other(lengths, frames, chips, beside, conv_grad, gain_rows, first, after):
    return pl.pallas_call(
        other_grad_kernel,
        out_shape=(rows_of((MORE, QUARTER), F32),) + (rows_of((MORE, QUARTER), BF16),) * 3,
        in_specs=[SMEM] + [VMEM] * 6 + [ANY],
        out_specs=(VMEM,) * 4,
        scratch_shapes=GRAD_SCRATCH + [pltpu.VMEM((MORE, WIDTH), F32)],
        compiler_params=LIMIT,
        cost_estimate=GRAD_COST,
        name="kernel_grads_other",
    )(lengths, frames, chips, beside, conv_grad, gain_rows, first, after)


def input_grad_kernel(lengths, conv_grad, outer, taps, _, out, token, g):
    where = where_of(lengths)
    token[...] = jnp.zeros(token.shape, F32)
    first, length = where[0], where[1]
    g[pl.ds(0, HALF), :] = outer[pl.ds(0, HALF), :].astype(F32)
    g[pl.ds(HALF, ROWS), :] = conv_grad[...].astype(F32)
    g[pl.ds(HALF + ROWS, HALF), :] = outer[pl.ds(HALF, HALF), :].astype(F32)

    def finish(total, begin):
        return masked_rows(total, first + begin, length).astype(BF16)

    depthwise(g, taps, out, ROWS, 64, finish, {j: KW - j for j in range(1, KW + 1)})


def input_grads(lengths, conv_grad, outer, taps, after):
    return pl.pallas_call(
        input_grad_kernel,
        out_shape=(rows_of((ROWS, WIDTH), BF16), rows_of((8, LANES), F32)),
        in_specs=[SMEM, VMEM, VMEM, VMEM, ANY],
        out_specs=(VMEM, VMEM),
        scratch_shapes=[pltpu.VMEM((ROWS + KW, WIDTH), F32)],
        compiler_params=LIMIT,
        cost_estimate=pl.CostEstimate(flops=50_000_000, bytes_accessed=2_000_000, transcendentals=0),
        name="input_grads",
    )(lengths, conv_grad, outer, taps, after)


def small_call(kernel, name, out_shape, operands, in_specs, scratch=()):
    return pl.pallas_call(
        kernel,
        out_shape=out_shape,
        in_specs=in_specs,
        out_specs=jax.tree.map(lambda _: VMEM, out_shape),
        scratch_shapes=list(scratch),
        compiler_params=LIMIT,
        cost_estimate=pl.CostEstimate(flops=500_000, bytes_accessed=1_500_000, transcendentals=0),
        name=name,
    )(*operands)


def row_products(place, hidden, hidden_other, cot, cot_other, step):
    columns = pl.ds(pl.multiple_of(place[1] * (WIDTH // 2), WIDTH // 2), WIDTH // 2)
    rows = pl.ds(pl.multiple_of(lax.rem(place[0] + step, 4) * QUARTER, QUARTER), QUARTER)
    dims = (((0,), (0,)), ((), ()))
    own_rows = pl.ds(HALF, ROWS)
    return lax.dot_general(
        hidden[own_rows, rows], cot[:, columns], dims, preferred_element_type=F32
    ) + lax.dot_general(hidden_other[own_rows, rows], cot_other[:, columns], dims, preferred_element_type=F32)


def far_kernel(hidden, hidden_other, cot, cot_other, _, far_a, far_b):
    place = place_of()
    value = row_products(place, hidden, hidden_other, cot, cot_other, 2).astype(BF16)
    far_a[...] = value[:, :QUARTER]
    far_b[...] = value[:, QUARTER:]


def far_products(hidden, hidden_other, cot, cot_other, after):
    half = rows_of((QUARTER, QUARTER), BF16)
    operands = (hidden, hidden_other, cot, cot_other, after)
    return small_call(far_kernel, "far_products", (half, half), operands, [VMEM] * 4 + [ANY])


def near_kernel(hidden, hidden_other, cot, cot_other, _, above_a, above_b, below_a, below_b, own):
    place = place_of()
    for step, (a, b) in ((1, (above_a, above_b)), (3, (below_a, below_b))):
        value = row_products(place, hidden, hidden_other, cot, cot_other, step)
        a[...] = value[:, :QUARTER].astype(a.dtype)
        b[...] = value[:, QUARTER:].astype(b.dtype)
    own[...] = row_products(place, hidden, hidden_other, cot, cot_other, 0)


def near_products(hidden, hidden_other, cot, cot_other, after):
    half = (QUARTER, QUARTER)
    shapes = tuple(rows_of(half, dtype) for dtype in (F32, BF16, BF16, F32)) + (rows_of((QUARTER, 2 * QUARTER), F32),)
    operands = (hidden, hidden_other, cot, cot_other, after)
    return small_call(near_kernel, "near_products", shapes, operands, [VMEM] * 4 + [ANY])


def seconds_kernel(above_a, up_a, below_b, down_b, _, second_a, second_b):
    second_a[...] = (above_a[...] + up_a[...].astype(F32)).astype(BF16)
    second_b[...] = (below_b[...] + down_b[...].astype(F32)).astype(BF16)


def seconds(above_a, up_a, below_b, down_b, after):
    return pl.pallas_call(
        seconds_kernel,
        out_shape=(rows_of((QUARTER, QUARTER), BF16),) * 2,
        in_specs=[VMEM, VMEM, VMEM, VMEM, ANY],
        out_specs=(VMEM,) * 2,
        compiler_params=LIMIT,
        cost_estimate=pl.CostEstimate(flops=300_000, bytes_accessed=2_400_000, transcendentals=0),
        name="seconds",
    )(above_a, up_a, below_b, down_b, after)


HALVES = 2 * BLOCK
HELD = (HALVES + EXTRA, WIDTH // 2)


def blocks_kernel(own, down_a, up_a, up_b, down_b, k0, k1, k2, k3, keep, send, total, extra):
    place = place_of()
    core = place[1]
    total[:, :QUARTER] = own[:, :QUARTER] + (down_a[...].astype(F32) + up_a[...].astype(F32))
    total[:, QUARTER:] = own[:, QUARTER:] + (down_b[...].astype(F32) + up_b[...].astype(F32))
    sums = k0[...] + (k1[...].astype(F32) + k2[...].astype(F32) + k3[...].astype(F32))
    extra[...] = jnp.zeros(extra.shape, F32)
    for z in range(2):
        for c in range(2):
            column = (2 * z + c) * BLOCK
            for q in range(5):
                value = sums[8 * q : 8 * q + 8, column : column + BLOCK]
                extra[c, pl.ds(8 * z, 8), pl.ds(q * BLOCK, BLOCK)] = value
    for out, c in ((keep, core), (send, 1 - core)):
        for z in range(2):
            rows = pl.ds(pl.multiple_of((2 * z + c) * BLOCK, BLOCK), BLOCK)
            out[pl.ds(z * BLOCK, BLOCK), :] = total[rows, :].astype(out.dtype)
        out[pl.ds(HALVES, EXTRA), :] = extra[c].astype(out.dtype)


def blocks(own, down_a, up_a, up_b, down_b, rows):
    return small_call(
        blocks_kernel,
        "blocks",
        (rows_of(HELD, F32), rows_of(HELD, BF16)),
        (own, down_a, up_a, up_b, down_b, *rows),
        [VMEM] * 9,
        [pltpu.VMEM((QUARTER, 2 * QUARTER), F32), pltpu.VMEM((2, EXTRA, WIDTH // 2), F32)],
    )


def chips_kernel(own, other, keep, send, extra):
    place = place_of()
    z_hi, core = place[2], place[1]
    more = pl.ds(HALVES, EXTRA)
    extra[...] = own[more, :] + other[more, :].astype(F32)
    for out, z in ((keep, z_hi), (send, 1 - z_hi)):
        rows = pl.ds(pl.multiple_of(z * BLOCK, BLOCK), BLOCK)
        out[pl.ds(pl.multiple_of(core * BLOCK, BLOCK), BLOCK), :] = own[rows, :].astype(out.dtype)
        out[pl.ds(pl.multiple_of((1 - core) * BLOCK, BLOCK), BLOCK), :] = other[rows, :].astype(out.dtype)
        value = extra[pl.ds(pl.multiple_of(8 * z, 8), 8), :]
        out[more, :] = jnp.concatenate([value, jnp.zeros((8, WIDTH // 2), F32)], axis=0).astype(out.dtype)


def chip_blocks(own, other):
    return small_call(
        chips_kernel,
        "chip_blocks",
        (rows_of(HELD, F32), rows_of(HELD, BF16)),
        (own, other),
        [VMEM, VMEM],
        [pltpu.VMEM((EXTRA, WIDTH // 2), F32)],
    )


def squares_kernel(mine, other, _, keep, one, two, three, square, extra):
    place = place_of()
    x = place[3]
    for half in range(2):
        rows = pl.ds(half * BLOCK, BLOCK)
        value = mine[rows, :] + other[rows, :].astype(F32)
        square[pl.ds(0, BLOCK), pl.ds(half * (WIDTH // 2), WIDTH // 2)] = value * value
    rows, more = pl.ds(HALVES, EXTRA), pl.ds(BLOCK, EXTRA)
    sums = mine[rows, :] + other[rows, :].astype(F32)
    extra[...] = sums * sums
    square[more, :] = jnp.zeros((EXTRA, WIDTH), F32)
    for dp in range(16):
        columns = pl.ds(dp * BLOCK, BLOCK)
        square[pl.ds(BLOCK, 2), columns] = extra[pl.ds(2 * (dp % 4), 2), pl.ds(dp // 4 * BLOCK, BLOCK)]
        square[pl.ds(BLOCK + 2, 1), columns] = extra[pl.ds(0, 1), pl.ds(4 * BLOCK, BLOCK)]
    for step, out in enumerate((keep, one, two, three)):
        columns = pl.ds(pl.multiple_of(lax.rem(x + step, 4) * QUARTER, QUARTER), QUARTER)
        out[...] = square[:, columns].astype(out.dtype)


def squares(mine, other, after):
    shape = (BLOCK + EXTRA, QUARTER)
    return small_call(
        squares_kernel,
        "squares",
        (rows_of(shape, F32),) + (rows_of(shape, BF16),) * 3,
        (mine, other, after),
        [VMEM, VMEM, ANY],
        [pltpu.VMEM((BLOCK + EXTRA, WIDTH), F32), pltpu.VMEM((EXTRA, WIDTH // 2), F32)],
    )


def quarters_kernel(keep, one, two, three, own, out_one, out_two, out_three, parts):
    place = place_of()
    z_lo = place[4]
    total = keep[...] + one[...].astype(F32) + two[...].astype(F32) + three[...].astype(F32)
    for z in range(4):
        parts[lax.rem(z - z_lo + 4, 4)] = total[:, z * BLOCK : (z + 1) * BLOCK]
    for step, out in enumerate((own, out_one, out_two, out_three)):
        out[...] = parts[step].astype(out.dtype)


def quarters(keep, one, two, three):
    shape = (BLOCK + EXTRA, BLOCK)
    return pl.pallas_call(
        quarters_kernel,
        out_shape=(rows_of(shape, F32),) + (rows_of(shape, BF16),) * 3,
        in_specs=[VMEM] * 4,
        out_specs=(VMEM,) * 4,
        scratch_shapes=[pltpu.VMEM((4,) + shape, F32)],
        compiler_params=LIMIT,
        cost_estimate=pl.CostEstimate(flops=1_000_000, bytes_accessed=1_000_000, transcendentals=0),
        name="quarters",
    )(keep, one, two, three)


def means_kernel(own, one, two, three, out, kernel, gain):
    total = own[...] + one[...].astype(F32) + two[...].astype(F32) + three[...].astype(F32)
    total = total * (1.0 / 16)
    out[...] = total[:BLOCK]
    kernel[...] = total[BLOCK : BLOCK + 2]
    gain[...] = total[BLOCK + 2 : BLOCK + 3]


def means(own, one, two, three):
    return pl.pallas_call(
        means_kernel,
        out_shape=(rows_of((BLOCK, BLOCK), F32), rows_of((2, BLOCK), F32), rows_of((1, BLOCK), F32)),
        in_specs=[VMEM] * 4,
        out_specs=(VMEM,) * 3,
        compiler_params=LIMIT,
        cost_estimate=pl.CostEstimate(flops=100_000, bytes_accessed=200_000, transcendentals=0),
        name="means",
    )(own, one, two, three)


def on_device(frames_in, cotangent, lengths, out_weight, conv_kernel, layer_norm_gain):
    seq = lax.axis_index("seq")
    core = seq % 2
    frames, cot = frames_in[0], cotangent[0]
    row = lax.broadcasted_iota(jnp.int32, (KW + 1, WIDTH), 0)
    taps = jnp.where(row < KW, jnp.pad(conv_kernel, ((0, 1), (0, 0))), layer_norm_gain[None])
    begin = jnp.concatenate([frames[: 2 * HALF], cot[:HALF]], axis=0)
    end = jnp.concatenate([frames[-2 * HALF :], cot[-HALF:]], axis=0)
    chips = move_neighbour(jnp.where(core == 0, begin, end))
    beside = move_core(jnp.where(core == 0, end, begin))
    cot_other = move_core(cot)
    forward = forward_inner(lengths, frames, taps)
    hidden, standard, inverse = forward_edge(lengths, frames, chips, beside, taps, forward)
    hidden_other = move_core(hidden)
    low = jnp.where(core == 0, chips[2 * HALF :], beside[2 * HALF :])
    high = jnp.where(core == 0, beside[2 * HALF :], chips[2 * HALF :])
    late_cot, _ = lax.optimization_barrier((jnp.concatenate([low, cot, high], axis=0), hidden))
    upstream = lax.dot_general(late_cot, out_weight, (((1,), (1,)), ((), ())), preferred_element_type=F32)
    operands = (hidden, hidden_other, cot, cot_other)
    far_a, far_b = far_products(*operands, upstream)
    above_a, above_b, below_a, below_b, own = near_products(*operands, far_a)
    up_a = move_y(far_a, 1)
    down_b = move_y(far_b, -1)
    up_b = move_y(above_b, 1)
    down_a = move_y(below_a, -1)
    conv_grad, gain_rows = backward(lengths, upstream, standard, inverse, taps, own)
    operands = (lengths, frames, chips, beside, conv_grad, gain_rows)
    rows = kernel_grads_first(*operands)
    second_a, second_b = seconds(above_a, up_a, below_b, down_b, rows)
    up_a = move_y(second_a, 1)
    down_b = move_y(second_b, -1)
    rows = kernel_grads_other(*operands, rows, second_a)
    rows = [rows[0]] + [move_y(rows[k], k) for k in (1, 2, 3)]
    own, other = blocks(own, down_a, up_a, up_b, down_b, rows)
    own, other = chip_blocks(own, move_core(other))
    outer = outer_grads(lengths, frames, chips, beside, taps, upstream, other)
    input_grad, token = input_grads(lengths, conv_grad, outer, taps, other)
    keep, *sent = squares(own, move_z_hi(other), token)
    keep, *sent = quarters(keep, *(move_x(value, k + 1) for k, value in enumerate(sent)))
    out, kernel, gain = means(keep, *(move_z_lo(value, k + 1) for k, value in enumerate(sent)))
    return input_grad[None], out, kernel, gain[0]


def solution(mesh):
    return jax.shard_map(
        on_device,
        mesh=mesh,
        in_specs=(P("dp", "seq", None), P("dp", "seq", None), P("dp"), P(), P(), P()),
        out_specs=(P("dp", "seq", None), P("seq", "dp"), P("dp", "seq"), P("seq")),
        check_vma=False,
    )
```

```python
import jax
import jax.numpy as jnp
from jax import lax
from jax.experimental import pallas as pl
from jax.experimental.pallas import tpu as pltpu
from jax.sharding import PartitionSpec as P

KW = 32
HALF = KW // 2
WIDTH = 1536
ROWS = 256
INNER = ROWS - 2 * HALF
LANES = 128
QUARTER = WIDTH // 4
BLOCK = WIDTH // 16
EXTRA = 16
MORE = 48
BF16, F32 = jnp.bfloat16, jnp.float32
SEQ = [(y, z, c) for y in range(4) for z in range(2) for c in range(2)]
DP = [(x, z) for x in range(4) for z in range(4)]
VMEM = pl.BlockSpec(memory_space=pltpu.VMEM)
SMEM = pl.BlockSpec(memory_space=pltpu.SMEM)
ANY = pl.BlockSpec(memory_space=pl.ANY)
LIMIT = pltpu.CompilerParams(vmem_limit_bytes=32 << 20)


def seq_at(y, z, c):
    return ((y % 4) * 2 + z % 2) * 2 + c % 2


def move_y(value, step):
    return lax.ppermute(value, "seq", [(seq_at(*p), seq_at(p[0] + step, p[1], p[2])) for p in SEQ])


def move_z_hi(value):
    return lax.ppermute(value, "seq", [(seq_at(*p), seq_at(p[0], p[1] + 1, p[2])) for p in SEQ])


def move_core(value):
    return lax.ppermute(value, "seq", [(seq_at(*p), seq_at(p[0], p[1], p[2] + 1)) for p in SEQ])


def move_x(value, step):
    return lax.ppermute(value, "dp", [(x * 4 + z, ((x + step) % 4) * 4 + z) for x, z in DP])


def move_z_lo(value, step):
    return lax.ppermute(value, "dp", [(x * 4 + z, x * 4 + (z + step) % 4) for x, z in DP])


def move_neighbour(value):
    return lax.ppermute(value, "seq", [(i, (i + 1) % 16 if i % 2 else (i - 1) % 16) for i in range(16)])


def place_of():
    seq, dp = lax.axis_index("seq"), lax.axis_index("dp")
    return seq >> 2, seq & 1, (seq >> 1) & 1, dp >> 2, dp & 3


def where_of(lengths):
    seq = lax.axis_index("seq")
    return seq * ROWS, lengths[0], seq & 1, seq >> 2


def masked_rows(rows, first, length):
    position = first + lax.broadcasted_iota(jnp.int32, rows.shape, 0)
    return jnp.where((position >= 0) & (position < length), rows.astype(F32), 0.0)


ALL = pl.ds(0, WIDTH)


def low_rows(core, chips, beside, begin, count, lanes=ALL):
    rows = pl.ds(begin, count)
    return jnp.where(core == 0, chips[rows, lanes].astype(F32), beside[rows, lanes].astype(F32))


def high_rows(core, chips, beside, begin, count, lanes=ALL):
    rows = pl.ds(begin, count)
    return jnp.where(core == 0, beside[rows, lanes].astype(F32), chips[rows, lanes].astype(F32))


def rows_of(shape, dtype):
    return jax.ShapeDtypeStruct(shape, dtype)


def rows_of(shape, dtype):
    return jax.ShapeDtypeStruct(shape, dtype)


def depthwise(x_ref, taps_ref, out_ref, rows, chunk, finish=None, taps=None, keep=None):
    taps = {j: j for j in range(KW)} if taps is None else taps

    def lane_block(i, carry):
        lanes = pl.ds(pl.multiple_of(i * LANES, LANES), LANES)
        for place, begin in enumerate(range(0, rows, chunk) if keep is None else keep):
            x = x_ref[pl.ds(begin, chunk + KW), lanes]
            total = None
            for shift in range(8):
                span = chunk if shift == 0 else chunk + 8
                sum_ = None
                for j in range(shift, KW + 1, 8):
                    if j in taps:
                        term = taps_ref[pl.ds(taps[j], 1), lanes] * x[j - shift : j - shift + span]
                        sum_ = term if sum_ is None else sum_ + term
                if shift:
                    sum_ = pltpu.roll(sum_, span - shift, 0)[:chunk]
                total = sum_ if total is None else total + sum_
            if finish is not None:
                total = finish(total, begin)
            out_ref[pl.ds(place * chunk, chunk), lanes] = total
        return carry

    lax.fori_loop(0, WIDTH // LANES, lane_block, 0)


LANE_BLOCKS = [pl.ds(i * LANES, LANES) for i in range(WIDTH // LANES)]


def row_sum(terms):
    total = None
    for term in terms:
        total = term if total is None else total + term
    return jnp.sum(total, axis=1, keepdims=True)


def standardise(conv, taps, refs, begin, size, offset, first, length):
    hidden, standard, inverse = refs
    rows, out = pl.ds(begin, size), pl.ds(offset, size)
    mean = row_sum(conv[rows, lanes] for lanes in LANE_BLOCKS) * (1.0 / WIDTH)
    variance = row_sum(jnp.square(conv[rows, lanes] - mean) for lanes in LANE_BLOCKS) * (1.0 / WIDTH)
    scale = lax.rsqrt(variance + 1e-05)
    valid = first + lax.broadcasted_iota(jnp.int32, (size, 1), 0) < length
    for lanes in LANE_BLOCKS:
        value = (conv[rows, lanes] - mean) * scale
        standard[out, lanes] = value
        if hidden is not None:
            normal = value * taps[pl.ds(KW, 1), lanes]
            value = normal * (0.5 + 0.5 * jnp.tanh(0.5 * normal))
            hidden[out, lanes] = jnp.where(valid, value, 0.0).astype(BF16)
    inverse[out, :] = jnp.broadcast_to(scale, (size, LANES))


def inner_kernel(lengths, frames, taps, hidden, standard, inverse, x, conv):
    where = where_of(lengths)
    first, length = where[0], where[1]
    x[...] = masked_rows(frames[...], first, length)
    depthwise(x, taps, conv, INNER, 112)
    for begin in range(0, INNER, 112):
        refs = (hidden, standard, inverse)
        standardise(conv, taps, refs, begin, 112, 2 * HALF + begin, first + HALF + begin, length)


def edge_kernel(lengths, top, bottom, chips, beside, taps, _, __, ___, ____, hidden, standard, inverse, x, conv, h, s, i):
    where = where_of(lengths)
    first, length, core = where[0], where[1], where[2]
    end = first + ROWS

    @pl.when(pl.program_id(0) == 0)
    def _both():
        x[pl.ds(0, HALF), :] = masked_rows(low_rows(core, chips, beside, HALF, HALF), first - HALF, length)
        x[pl.ds(HALF, 2 * HALF), :] = masked_rows(top[...], first, length)
        x[pl.ds(3 * HALF, 2 * HALF), :] = masked_rows(bottom[...], end - 2 * HALF, length)
        x[pl.ds(5 * HALF, HALF), :] = masked_rows(high_rows(core, chips, beside, 0, HALF), end, length)
        depthwise(x, taps, conv, 4 * HALF, HALF, keep=(0, 3 * HALF))
        standardise(conv, taps, (h, s, i), 0, HALF, 0, first, length)
        standardise(conv, taps, (h, s, i), HALF, HALF, HALF, end - HALF, length)

    rows = pl.ds(pl.multiple_of(pl.program_id(0) * HALF, HALF), HALF)
    hidden[...] = h[rows, :]
    standard[...] = s[rows, :]
    inverse[...] = i[rows, :]


SPAN = ROWS + 2 * HALF
FORWARD = (rows_of((SPAN, WIDTH), BF16), rows_of((SPAN, WIDTH), F32), rows_of((SPAN, LANES), F32))


def forward_inner(lengths, frames, taps):
    return pl.pallas_call(
        inner_kernel,
        out_shape=FORWARD,
        in_specs=[SMEM, VMEM, VMEM],
        out_specs=(VMEM, VMEM, VMEM),
        scratch_shapes=[pltpu.VMEM((ROWS, WIDTH), F32), pltpu.VMEM((INNER, WIDTH), F32)],
        compiler_params=LIMIT,
        cost_estimate=pl.CostEstimate(flops=60_000_000, bytes_accessed=4_000_000, transcendentals=800_000),
        name="forward_inner",
    )(lengths, frames, taps)


def fixed(shape, row=0):
    return pl.BlockSpec(shape, lambda i: (row, 0))


SIDE = fixed((3 * HALF, WIDTH))
SCRATCH = [pltpu.VMEM((6 * HALF, WIDTH), F32), pltpu.VMEM((2 * HALF, WIDTH), F32)]
KEPT = [pltpu.VMEM((2 * HALF, WIDTH), BF16), pltpu.VMEM((2 * HALF, WIDTH), F32), pltpu.VMEM((2 * HALF, LANES), F32)]


def forward_edge(lengths, frames, chips, beside, taps, forward, after):
    def ends(i):
        return (1 + 15 * i, 0)

    return pl.pallas_call(
        edge_kernel,
        grid=(2,),
        out_shape=FORWARD,
        in_specs=[
            SMEM,
            fixed((2 * HALF, WIDTH)),
            fixed((2 * HALF, WIDTH), 7),
            SIDE,
            SIDE,
            fixed((KW + 1, WIDTH)),
            ANY,
            ANY,
            ANY,
            ANY,
        ],
        out_specs=(
            pl.BlockSpec((HALF, WIDTH), ends),
            pl.BlockSpec((HALF, WIDTH), ends),
            pl.BlockSpec((HALF, LANES), ends),
        ),
        scratch_shapes=SCRATCH + KEPT,
        input_output_aliases={6: 0, 7: 1, 8: 2},
        compiler_params=LIMIT,
        cost_estimate=pl.CostEstimate(flops=8_000_000, bytes_accessed=1_000_000, transcendentals=100_000),
        name="forward_edge",
    )(lengths, frames, frames, chips, beside, taps, *forward, after)


def backward_rows(first, length, upstream, begin, standard, row, inverse, taps, conv_grad, out_row, size, scaled):
    source, rows, held, out = pl.ds(begin, size), pl.ds(row, size), pl.ds(0, size), pl.ds(out_row, size)
    position = first + lax.broadcasted_iota(jnp.int32, (size, 1), 0)
    valid = (position >= 0) & (position < length)
    means, slopes, terms = None, None, []
    for lanes in LANE_BLOCKS:
        value = standard[rows, lanes]
        gain = taps[pl.ds(KW, 1), lanes]
        normal = value * gain
        sigma = 0.5 + 0.5 * jnp.tanh(0.5 * normal)
        grad = jnp.where(valid, upstream[source, lanes] * (sigma + normal * sigma * (1.0 - sigma)), 0.0)
        terms.append(jnp.sum((grad * value).reshape(size // 8, 8, LANES), axis=0))
        grad = grad * gain
        scaled[held, lanes] = grad
        slope = grad * value
        means = grad if means is None else means + grad
        slopes = slope if slopes is None else slopes + slope
    mean = jnp.sum(means, axis=1, keepdims=True) * (1.0 / WIDTH)
    slope = jnp.sum(slopes, axis=1, keepdims=True) * (1.0 / WIDTH)
    scale = inverse[rows, :1]
    for lanes in LANE_BLOCKS:
        value = scaled[held, lanes] - mean - standard[rows, lanes] * slope
        conv_grad[out, lanes] = (scale * value).astype(BF16)
    return terms


def backward_kernel(lengths, upstream, standard, inverse, taps, _, conv_grad, gain_sum, scaled):
    where = where_of(lengths)
    terms = []
    for begin in (0, ROWS // 2):
        span = HALF + begin
        refs = (upstream, span, standard, span, inverse, taps, conv_grad, begin, ROWS // 2, scaled)
        terms.append(backward_rows(where[0] + begin, where[1], *refs))
    for lanes, one, two in zip(LANE_BLOCKS, *terms):
        gain_sum[:, lanes] = one + two


def backward(lengths, upstream, standard, inverse, taps, after):
    return pl.pallas_call(
        backward_kernel,
        out_shape=(rows_of((ROWS, WIDTH), BF16), rows_of((8, WIDTH), F32)),
        in_specs=[SMEM, VMEM, VMEM, VMEM, VMEM, ANY],
        out_specs=(VMEM, VMEM),
        scratch_shapes=[pltpu.VMEM((ROWS // 2, WIDTH), F32)],
        compiler_params=LIMIT,
        cost_estimate=pl.CostEstimate(flops=10_000_000, bytes_accessed=4_000_000, transcendentals=400_000),
        name="backward",
    )(lengths, upstream, standard, inverse, taps, after)


def outer_kernel(lengths, frames, chips, beside, taps, upstream, _, out, x, conv, standard, inverse, scaled):
    where = where_of(lengths)
    first, length, core = where[0], where[1], where[2]
    end = first + ROWS
    top, bottom = frames[pl.ds(0, HALF), :], frames[pl.ds(ROWS - HALF, HALF), :]
    x[pl.ds(0, 2 * HALF), :] = masked_rows(low_rows(core, chips, beside, 0, 2 * HALF), first - 2 * HALF, length)
    x[pl.ds(2 * HALF, HALF), :] = masked_rows(top, first, length)
    x[pl.ds(3 * HALF, HALF), :] = masked_rows(bottom, end - HALF, length)
    x[pl.ds(4 * HALF, 2 * HALF), :] = masked_rows(high_rows(core, chips, beside, 0, 2 * HALF), end, length)
    depthwise(x, taps, conv, 4 * HALF, HALF, keep=(0, 3 * HALF))
    standardise(conv, taps, (None, standard, inverse), 0, 2 * HALF, 0, first, length)
    for row, begin, position in ((0, 0, first - HALF), (HALF, HALF + ROWS, end)):
        refs = (upstream, begin, standard, row, inverse, taps, out, row, HALF, scaled)
        backward_rows(position, length, *refs)


def outer_grads(lengths, frames, chips, beside, taps, upstream, after):
    return pl.pallas_call(
        outer_kernel,
        out_shape=rows_of((2 * HALF, WIDTH), BF16),
        in_specs=[SMEM] + [VMEM] * 5 + [ANY],
        out_specs=VMEM,
        scratch_shapes=SCRATCH + KEPT[1:] + [pltpu.VMEM((HALF, WIDTH), F32)],
        compiler_params=LIMIT,
        cost_estimate=pl.CostEstimate(flops=8_000_000, bytes_accessed=1_000_000, transcendentals=0),
        name="outer_grads",
    )(lengths, frames, chips, beside, taps, upstream, after)


SIDE_LANES = WIDTH // 2


def fill_rows(where, frames, chips, beside, conv_grad, x, g, columns):
    first, length, core = where[0], where[1], where[2]
    low = low_rows(core, chips, beside, HALF, HALF, columns)
    high = high_rows(core, chips, beside, 0, HALF, columns)
    x[pl.ds(0, HALF), :] = masked_rows(low, first - HALF, length)
    x[pl.ds(HALF, ROWS), :] = masked_rows(frames[:, columns], first, length)
    x[pl.ds(HALF + ROWS, HALF), :] = masked_rows(high, first + ROWS, length)
    g[pl.ds(0, 8), :] = jnp.zeros((8, SIDE_LANES), F32)
    g[pl.ds(8, ROWS), :] = conv_grad[:, columns].astype(F32)
    g[pl.ds(8 + ROWS, 8), :] = jnp.zeros((8, SIDE_LANES), F32)


def kernel_grad_lanes(x, g, gain_rows, out, offset):
    chunk = 88

    def lane_block(i, carry):
        lanes = pl.ds(pl.multiple_of(i * LANES, LANES), LANES)
        whole = pl.ds(pl.multiple_of(i * LANES + offset, LANES), LANES)
        sums = [None] * KW
        for begin in range(0, ROWS + 8, chunk):
            x_rows = x[pl.ds(begin, chunk + KW - 8), lanes]
            grad = g[pl.ds(begin, chunk + 8), lanes]
            for shift in range(8):
                moved = grad[8:] if shift == 0 else pltpu.roll(grad, shift, 0)[8:]
                for a in range(KW // 8):
                    j = 8 * a + shift
                    product = (moved * x_rows[8 * a : 8 * a + chunk]).reshape(chunk // 8, 8, LANES)
                    product = jnp.sum(product, axis=0)
                    sums[j] = product if sums[j] is None else sums[j] + product
        out[pl.ds(0, KW), whole] = jnp.concatenate(
            [jnp.sum(value, axis=0, keepdims=True) for value in sums], axis=0
        )
        gain = jnp.sum(gain_rows[:, whole], axis=0, keepdims=True)
        out[pl.ds(KW, 8), whole] = jnp.broadcast_to(gain, (8, LANES))
        return carry

    lax.fori_loop(0, SIDE_LANES // LANES, lane_block, 0)


def first_grad_kernel(lengths, frames, chips, beside, conv_grad, gain_rows, out, x, g):
    where = where_of(lengths)
    fill_rows(where, frames, chips, beside, conv_grad, x, g, pl.ds(0, SIDE_LANES))
    kernel_grad_lanes(x, g, gain_rows, out, 0)


def other_grad_kernel(lengths, frames, chips, beside, conv_grad, gain_rows, first, _, keep, one, two, three, x, g, rows):
    where = where_of(lengths)
    fill_rows(where, frames, chips, beside, conv_grad, x, g, pl.ds(SIDE_LANES, SIDE_LANES))
    rows[pl.ds(0, KW + 8), pl.ds(0, SIDE_LANES)] = first[...]
    kernel_grad_lanes(x, g, gain_rows, rows, SIDE_LANES)
    rows[pl.ds(KW + 8, 8), :] = jnp.zeros((8, WIDTH), F32)
    for step, out in enumerate((keep, one, two, three)):
        columns = pl.ds(pl.multiple_of(lax.rem(where[3] + step, 4) * QUARTER, QUARTER), QUARTER)
        out[...] = rows[:, columns].astype(out.dtype)


GRAD_SCRATCH = [pltpu.VMEM((ROWS + KW, SIDE_LANES), F32), pltpu.VMEM((ROWS + 16, SIDE_LANES), F32)]
GRAD_COST = pl.CostEstimate(flops=25_000_000, bytes_accessed=1_000_000, transcendentals=0)


def kernel_grads_first(lengths, frames, chips, beside, conv_grad, gain_rows):
    return pl.pallas_call(
        first_grad_kernel,
        out_shape=rows_of((KW + 8, SIDE_LANES), F32),
        in_specs=[SMEM] + [VMEM] * 5,
        out_specs=VMEM,
        scratch_shapes=GRAD_SCRATCH,
        compiler_params=LIMIT,
        cost_estimate=GRAD_COST,
        name="kernel_grads_first",
    )(lengths, frames, chips, beside, conv_grad, gain_rows)


def kernel_grads_other(lengths, frames, chips, beside, conv_grad, gain_rows, first, after):
    return pl.pallas_call(
        other_grad_kernel,
        out_shape=(rows_of((MORE, QUARTER), F32),) + (rows_of((MORE, QUARTER), BF16),) * 3,
        in_specs=[SMEM] + [VMEM] * 6 + [ANY],
        out_specs=(VMEM,) * 4,
        scratch_shapes=GRAD_SCRATCH + [pltpu.VMEM((MORE, WIDTH), F32)],
        compiler_params=LIMIT,
        cost_estimate=GRAD_COST,
        name="kernel_grads_other",
    )(lengths, frames, chips, beside, conv_grad, gain_rows, first, after)


def input_grad_kernel(lengths, conv_grad, outer, taps, _, out, token, g):
    where = where_of(lengths)
    token[...] = jnp.zeros(token.shape, F32)
    first, length = where[0], where[1]
    g[pl.ds(0, HALF), :] = outer[pl.ds(0, HALF), :].astype(F32)
    g[pl.ds(HALF, ROWS), :] = conv_grad[...].astype(F32)
    g[pl.ds(HALF + ROWS, HALF), :] = outer[pl.ds(HALF, HALF), :].astype(F32)

    def finish(total, begin):
        return masked_rows(total, first + begin, length).astype(BF16)

    depthwise(g, taps, out, ROWS, 64, finish, {j: KW - j for j in range(1, KW + 1)})


def input_grads(lengths, conv_grad, outer, taps, after):
    return pl.pallas_call(
        input_grad_kernel,
        out_shape=(rows_of((ROWS, WIDTH), BF16), rows_of((8, LANES), F32)),
        in_specs=[SMEM, VMEM, VMEM, VMEM, ANY],
        out_specs=(VMEM, VMEM),
        scratch_shapes=[pltpu.VMEM((ROWS + KW, WIDTH), F32)],
        compiler_params=LIMIT,
        cost_estimate=pl.CostEstimate(flops=50_000_000, bytes_accessed=2_000_000, transcendentals=0),
        name="input_grads",
    )(lengths, conv_grad, outer, taps, after)


def small_call(kernel, name, out_shape, operands, in_specs, scratch=()):
    return pl.pallas_call(
        kernel,
        out_shape=out_shape,
        in_specs=in_specs,
        out_specs=jax.tree.map(lambda _: VMEM, out_shape),
        scratch_shapes=list(scratch),
        compiler_params=LIMIT,
        cost_estimate=pl.CostEstimate(flops=500_000, bytes_accessed=1_500_000, transcendentals=0),
        name=name,
    )(*operands)


def row_products(place, hidden, hidden_other, cot, cot_other, step):
    columns = pl.ds(pl.multiple_of(place[1] * (WIDTH // 2), WIDTH // 2), WIDTH // 2)
    rows = pl.ds(pl.multiple_of(lax.rem(place[0] + step, 4) * QUARTER, QUARTER), QUARTER)
    dims = (((0,), (0,)), ((), ()))
    own_rows = pl.ds(HALF, ROWS)
    return lax.dot_general(
        hidden[own_rows, rows], cot[:, columns], dims, preferred_element_type=F32
    ) + lax.dot_general(hidden_other[own_rows, rows], cot_other[:, columns], dims, preferred_element_type=F32)


def far_kernel(hidden, hidden_other, cot, cot_other, _, far_a, far_b):
    place = place_of()
    value = row_products(place, hidden, hidden_other, cot, cot_other, 2).astype(BF16)
    far_a[...] = value[:, :QUARTER]
    far_b[...] = value[:, QUARTER:]


def far_products(hidden, hidden_other, cot, cot_other, after):
    half = rows_of((QUARTER, QUARTER), BF16)
    operands = (hidden, hidden_other, cot, cot_other, after)
    return small_call(far_kernel, "far_products", (half, half), operands, [VMEM] * 4 + [ANY])


def near_kernel(hidden, hidden_other, cot, cot_other, _, above_a, above_b, below_a, below_b, own):
    place = place_of()
    for step, (a, b) in ((1, (above_a, above_b)), (3, (below_a, below_b))):
        value = row_products(place, hidden, hidden_other, cot, cot_other, step)
        a[...] = value[:, :QUARTER].astype(a.dtype)
        b[...] = value[:, QUARTER:].astype(b.dtype)
    own[...] = row_products(place, hidden, hidden_other, cot, cot_other, 0)


def near_products(hidden, hidden_other, cot, cot_other, after):
    half = (QUARTER, QUARTER)
    shapes = tuple(rows_of(half, dtype) for dtype in (F32, BF16, BF16, F32)) + (rows_of((QUARTER, 2 * QUARTER), F32),)
    operands = (hidden, hidden_other, cot, cot_other, after)
    return small_call(near_kernel, "near_products", shapes, operands, [VMEM] * 4 + [ANY])


def seconds_kernel(above_a, up_a, below_b, down_b, _, second_a, second_b):
    second_a[...] = (above_a[...] + up_a[...].astype(F32)).astype(BF16)
    second_b[...] = (below_b[...] + down_b[...].astype(F32)).astype(BF16)


def seconds(above_a, up_a, below_b, down_b, after):
    return pl.pallas_call(
        seconds_kernel,
        out_shape=(rows_of((QUARTER, QUARTER), BF16),) * 2,
        in_specs=[VMEM, VMEM, VMEM, VMEM, ANY],
        out_specs=(VMEM,) * 2,
        compiler_params=LIMIT,
        cost_estimate=pl.CostEstimate(flops=300_000, bytes_accessed=2_400_000, transcendentals=0),
        name="seconds",
    )(above_a, up_a, below_b, down_b, after)


HALVES = 2 * BLOCK
HELD = (HALVES + EXTRA, WIDTH // 2)


def blocks_kernel(own, down_a, up_a, up_b, down_b, k0, k1, k2, k3, keep, send, total, extra):
    place = place_of()
    core = place[1]
    total[:, :QUARTER] = own[:, :QUARTER] + (down_a[...].astype(F32) + up_a[...].astype(F32))
    total[:, QUARTER:] = own[:, QUARTER:] + (down_b[...].astype(F32) + up_b[...].astype(F32))
    sums = k0[...] + (k1[...].astype(F32) + k2[...].astype(F32) + k3[...].astype(F32))
    extra[...] = jnp.zeros(extra.shape, F32)
    for z in range(2):
        for c in range(2):
            column = (2 * z + c) * BLOCK
            for q in range(5):
                value = sums[8 * q : 8 * q + 8, column : column + BLOCK]
                extra[c, pl.ds(8 * z, 8), pl.ds(q * BLOCK, BLOCK)] = value
    for out, c in ((keep, core), (send, 1 - core)):
        for z in range(2):
            rows = pl.ds(pl.multiple_of((2 * z + c) * BLOCK, BLOCK), BLOCK)
            out[pl.ds(z * BLOCK, BLOCK), :] = total[rows, :].astype(out.dtype)
        out[pl.ds(HALVES, EXTRA), :] = extra[c].astype(out.dtype)


def blocks(own, down_a, up_a, up_b, down_b, rows):
    return small_call(
        blocks_kernel,
        "blocks",
        (rows_of(HELD, F32), rows_of(HELD, BF16)),
        (own, down_a, up_a, up_b, down_b, *rows),
        [VMEM] * 9,
        [pltpu.VMEM((QUARTER, 2 * QUARTER), F32), pltpu.VMEM((2, EXTRA, WIDTH // 2), F32)],
    )


PIECE = BLOCK // 2
PACKED = (PIECE, 4 * (WIDTH // 2) + LANES)
TAIL = pl.ds(4 * (WIDTH // 2), LANES)


def chips_kernel(own, other, keep, send, extra, tail):
    place = place_of()
    z_hi, core, half = place[2], place[1], WIDTH // 2
    more = pl.ds(HALVES, EXTRA)
    extra[...] = own[more, :] + other[more, :].astype(F32)
    for out, z in ((keep, z_hi), (send, 1 - z_hi)):
        for source, c in ((own, core), (other, 1 - core)):
            for i in range(2):
                rows = pl.ds(pl.multiple_of(z * BLOCK + i * PIECE, PIECE), PIECE)
                columns = pl.ds(pl.multiple_of((2 * c + i) * half, half), half)
                out[:, columns] = source[rows, :].astype(out.dtype)
        tail[...] = jnp.zeros(tail.shape, F32)
        rows = pl.ds(pl.multiple_of(8 * z, 8), 8)
        for q in range(5):
            tail[pl.ds(8 * q, 8), pl.ds(0, BLOCK)] = extra[rows, pl.ds(q * BLOCK, BLOCK)]
        out[:, TAIL] = tail[...].astype(out.dtype)


def chip_blocks(own, other):
    return small_call(
        chips_kernel,
        "chip_blocks",
        (rows_of(PACKED, F32), rows_of(PACKED, BF16)),
        (own, other),
        [VMEM, VMEM],
        [pltpu.VMEM((EXTRA, WIDTH // 2), F32), pltpu.VMEM((PIECE, LANES), F32)],
    )


def squares_kernel(mine, other, _, keep, one, two, three, square, extra):
    x, half = lax.axis_index("dp") >> 2, WIDTH // 2
    for block in range(4):
        columns = pl.ds(block * half, half)
        value = mine[:, columns] + other[:, columns].astype(F32)
        square[pl.ds(block % 2 * PIECE, PIECE), pl.ds(block // 2 * half, half)] = value * value
    sums = mine[:, TAIL] + other[:, TAIL].astype(F32)
    extra[...] = sums * sums
    square[pl.ds(BLOCK, EXTRA), :] = jnp.zeros((EXTRA, WIDTH), F32)
    for dp in range(16):
        columns = pl.ds(dp * BLOCK, BLOCK)
        square[pl.ds(BLOCK, 2), columns] = extra[pl.ds(2 * dp, 2), pl.ds(0, BLOCK)]
        square[pl.ds(BLOCK + 2, 1), columns] = extra[pl.ds(KW, 1), pl.ds(0, BLOCK)]
    for step, out in enumerate((keep, one, two, three)):
        columns = pl.ds(pl.multiple_of(lax.rem(x + step, 4) * QUARTER, QUARTER), QUARTER)
        out[...] = square[:, columns].astype(out.dtype)


def squares(mine, other, after):
    shape = (BLOCK + EXTRA, QUARTER)
    return small_call(
        squares_kernel,
        "squares",
        (rows_of(shape, F32),) + (rows_of(shape, BF16),) * 3,
        (mine, other, after),
        [VMEM, VMEM, ANY],
        [pltpu.VMEM((BLOCK + EXTRA, WIDTH), F32), pltpu.VMEM((PIECE, LANES), F32)],
    )


def quarters_kernel(keep, one, two, three, own, out_one, out_two, out_three, parts):
    place = place_of()
    z_lo = place[4]
    total = keep[...] + one[...].astype(F32) + two[...].astype(F32) + three[...].astype(F32)
    for z in range(4):
        parts[lax.rem(z - z_lo + 4, 4)] = total[:, z * BLOCK : (z + 1) * BLOCK]
    for step, out in enumerate((own, out_one, out_two, out_three)):
        out[...] = parts[step].astype(out.dtype)


def quarters(keep, one, two, three):
    shape = (BLOCK + EXTRA, BLOCK)
    return pl.pallas_call(
        quarters_kernel,
        out_shape=(rows_of(shape, F32),) + (rows_of(shape, BF16),) * 3,
        in_specs=[VMEM] * 4,
        out_specs=(VMEM,) * 4,
        scratch_shapes=[pltpu.VMEM((4,) + shape, F32)],
        compiler_params=LIMIT,
        cost_estimate=pl.CostEstimate(flops=1_000_000, bytes_accessed=1_000_000, transcendentals=0),
        name="quarters",
    )(keep, one, two, three)


def means_kernel(own, one, two, three, out, kernel, gain):
    total = own[...] + one[...].astype(F32) + two[...].astype(F32) + three[...].astype(F32)
    total = total * (1.0 / 16)
    out[...] = total[:BLOCK]
    kernel[...] = total[BLOCK : BLOCK + 2]
    gain[...] = total[BLOCK + 2 : BLOCK + 3]


def means(own, one, two, three):
    return pl.pallas_call(
        means_kernel,
        out_shape=(rows_of((BLOCK, BLOCK), F32), rows_of((2, BLOCK), F32), rows_of((1, BLOCK), F32)),
        in_specs=[VMEM] * 4,
        out_specs=(VMEM,) * 3,
        compiler_params=LIMIT,
        cost_estimate=pl.CostEstimate(flops=100_000, bytes_accessed=200_000, transcendentals=0),
        name="means",
    )(own, one, two, three)


def on_device(frames_in, cotangent, lengths, out_weight, conv_kernel, layer_norm_gain):
    seq = lax.axis_index("seq")
    core = seq % 2
    frames, cot = frames_in[0], cotangent[0]
    row = lax.broadcasted_iota(jnp.int32, (KW + 1, WIDTH), 0)
    taps = jnp.where(row < KW, jnp.pad(conv_kernel, ((0, 1), (0, 0))), layer_norm_gain[None])
    begin = jnp.concatenate([frames[: 2 * HALF], cot[:HALF]], axis=0)
    end = jnp.concatenate([frames[-2 * HALF :], cot[-HALF:]], axis=0)
    chips = move_neighbour(jnp.where(core == 0, begin, end))
    beside = move_core(jnp.where(core == 0, end, begin))
    cot_other = move_core(cot)
    forward = forward_inner(lengths, frames, taps)
    hidden, standard, inverse = forward_edge(lengths, frames, chips, beside, taps, forward, cot_other)
    hidden_other = move_core(hidden)
    low = jnp.where(core == 0, chips[2 * HALF :], beside[2 * HALF :])
    high = jnp.where(core == 0, beside[2 * HALF :], chips[2 * HALF :])
    operands = (hidden, hidden_other, cot, cot_other)
    far_a, far_b = far_products(*operands, low)
    late_cot, far_a, far_b = lax.optimization_barrier((jnp.concatenate([low, cot, high], axis=0), far_a, far_b))
    upstream = lax.dot_general(late_cot, out_weight, (((1,), (1,)), ((), ())), preferred_element_type=F32)
    above_a, above_b, below_a, below_b, own = near_products(*operands, upstream)
    up_a = move_y(far_a, 1)
    down_b = move_y(far_b, -1)
    up_b = move_y(above_b, 1)
    down_a = move_y(below_a, -1)
    conv_grad, gain_rows = backward(lengths, upstream, standard, inverse, taps, own)
    operands = (lengths, frames, chips, beside, conv_grad, gain_rows)
    rows = kernel_grads_first(*operands)
    second_a, second_b = seconds(above_a, up_a, below_b, down_b, rows)
    up_a = move_y(second_a, 1)
    down_b = move_y(second_b, -1)
    rows = kernel_grads_other(*operands, rows, second_a)
    rows = [rows[0]] + [move_y(rows[k], k) for k in (1, 2, 3)]
    own, other = blocks(own, down_a, up_a, up_b, down_b, rows)
    own, other = chip_blocks(own, move_core(other))
    outer = outer_grads(lengths, frames, chips, beside, taps, upstream, other)
    input_grad, token = input_grads(lengths, conv_grad, outer, taps, other)
    keep, *sent = squares(own, move_z_hi(other), token)
    keep, *sent = quarters(keep, *(move_x(value, k + 1) for k, value in enumerate(sent)))
    out, kernel, gain = means(keep, *(move_z_lo(value, k + 1) for k, value in enumerate(sent)))
    return input_grad[None], out, kernel, gain[0]


def solution(mesh):
    return jax.shard_map(
        on_device,
        mesh=mesh,
        in_specs=(P("dp", "seq", None), P("dp", "seq", None), P("dp"), P(), P(), P()),
        out_specs=(P("dp", "seq", None), P("seq", "dp"), P("dp", "seq"), P("seq")),
        check_vma=False,
    )
```

```python
import jax
import jax.numpy as jnp
from jax import lax
from jax.experimental import pallas as pl
from jax.experimental.pallas import tpu as pltpu
from jax.sharding import PartitionSpec as P

KW = 32
HALF = KW // 2
WIDTH = 1536
ROWS = 256
INNER = ROWS - 2 * HALF
LANES = 128
QUARTER = WIDTH // 4
BLOCK = WIDTH // 16
EXTRA = 16
MORE = 48
BF16, F32 = jnp.bfloat16, jnp.float32
SEQ = [(y, z, c) for y in range(4) for z in range(2) for c in range(2)]
DP = [(x, z) for x in range(4) for z in range(4)]
VMEM = pl.BlockSpec(memory_space=pltpu.VMEM)
SMEM = pl.BlockSpec(memory_space=pltpu.SMEM)
ANY = pl.BlockSpec(memory_space=pl.ANY)
LIMIT = pltpu.CompilerParams(vmem_limit_bytes=32 << 20)


def seq_at(y, z, c):
    return ((y % 4) * 2 + z % 2) * 2 + c % 2


def move_y(value, step):
    return lax.ppermute(value, "seq", [(seq_at(*p), seq_at(p[0] + step, p[1], p[2])) for p in SEQ])


def move_z_hi(value):
    return lax.ppermute(value, "seq", [(seq_at(*p), seq_at(p[0], p[1] + 1, p[2])) for p in SEQ])


def move_core(value):
    return lax.ppermute(value, "seq", [(seq_at(*p), seq_at(p[0], p[1], p[2] + 1)) for p in SEQ])


def move_x(value, step):
    return lax.ppermute(value, "dp", [(x * 4 + z, ((x + step) % 4) * 4 + z) for x, z in DP])


def move_z_lo(value, step):
    return lax.ppermute(value, "dp", [(x * 4 + z, x * 4 + (z + step) % 4) for x, z in DP])


def move_neighbour(value):
    return lax.ppermute(value, "seq", [(i, (i + 1) % 16 if i % 2 else (i - 1) % 16) for i in range(16)])


def place_of():
    seq, dp = lax.axis_index("seq"), lax.axis_index("dp")
    return seq >> 2, seq & 1, (seq >> 1) & 1, dp >> 2, dp & 3


def where_of(lengths):
    seq = lax.axis_index("seq")
    return seq * ROWS, lengths[0], seq & 1, seq >> 2


def masked_rows(rows, first, length):
    position = first + lax.broadcasted_iota(jnp.int32, rows.shape, 0)
    return jnp.where((position >= 0) & (position < length), rows.astype(F32), 0.0)


ALL = pl.ds(0, WIDTH)


def low_rows(core, chips, beside, begin, count, lanes=ALL):
    rows = pl.ds(begin, count)
    return jnp.where(core == 0, chips[rows, lanes].astype(F32), beside[rows, lanes].astype(F32))


def high_rows(core, chips, beside, begin, count, lanes=ALL):
    rows = pl.ds(begin, count)
    return jnp.where(core == 0, beside[rows, lanes].astype(F32), chips[rows, lanes].astype(F32))


def rows_of(shape, dtype):
    return jax.ShapeDtypeStruct(shape, dtype)


def rows_of(shape, dtype):
    return jax.ShapeDtypeStruct(shape, dtype)


def depthwise(x_ref, taps_ref, out_ref, rows, chunk, finish=None, taps=None, keep=None):
    taps = {j: j for j in range(KW)} if taps is None else taps

    def lane_block(i, carry):
        lanes = pl.ds(pl.multiple_of(i * LANES, LANES), LANES)
        for place, begin in enumerate(range(0, rows, chunk) if keep is None else keep):
            x = x_ref[pl.ds(begin, chunk + KW), lanes]
            total = None
            for shift in range(8):
                span = chunk if shift == 0 else chunk + 8
                sum_ = None
                for j in range(shift, KW + 1, 8):
                    if j in taps:
                        term = taps_ref[pl.ds(taps[j], 1), lanes] * x[j - shift : j - shift + span]
                        sum_ = term if sum_ is None else sum_ + term
                if shift:
                    sum_ = pltpu.roll(sum_, span - shift, 0)[:chunk]
                total = sum_ if total is None else total + sum_
            if finish is not None:
                total = finish(total, begin)
            out_ref[pl.ds(place * chunk, chunk), lanes] = total
        return carry

    lax.fori_loop(0, WIDTH // LANES, lane_block, 0)


LANE_BLOCKS = [pl.ds(i * LANES, LANES) for i in range(WIDTH // LANES)]


def row_sum(terms):
    total = None
    for term in terms:
        total = term if total is None else total + term
    return jnp.sum(total, axis=1, keepdims=True)


def standardise(conv, taps, refs, begin, size, offset, first, length):
    hidden, standard, inverse = refs
    rows, out = pl.ds(begin, size), pl.ds(offset, size)
    mean = row_sum(conv[rows, lanes] for lanes in LANE_BLOCKS) * (1.0 / WIDTH)
    variance = row_sum(jnp.square(conv[rows, lanes] - mean) for lanes in LANE_BLOCKS) * (1.0 / WIDTH)
    scale = lax.rsqrt(variance + 1e-05)
    valid = first + lax.broadcasted_iota(jnp.int32, (size, 1), 0) < length
    for lanes in LANE_BLOCKS:
        value = (conv[rows, lanes] - mean) * scale
        standard[out, lanes] = value
        if hidden is not None:
            normal = value * taps[pl.ds(KW, 1), lanes]
            value = normal * (0.5 + 0.5 * jnp.tanh(0.5 * normal))
            hidden[out, lanes] = jnp.where(valid, value, 0.0).astype(BF16)
    inverse[out, :] = jnp.broadcast_to(scale, (size, LANES))


def inner_kernel(lengths, frames, taps, hidden, standard, inverse, x, conv):
    where = where_of(lengths)
    first, length = where[0], where[1]
    x[...] = masked_rows(frames[...], first, length)
    depthwise(x, taps, conv, INNER, 112)
    for begin in range(0, INNER, 112):
        refs = (hidden, standard, inverse)
        standardise(conv, taps, refs, begin, 112, 2 * HALF + begin, first + HALF + begin, length)


def edge_kernel(lengths, top, bottom, chips, beside, taps, _, __, ___, hidden, standard, inverse, x, conv, h, s, i):
    where = where_of(lengths)
    first, length, core = where[0], where[1], where[2]
    end = first + ROWS

    @pl.when(pl.program_id(0) == 0)
    def _both():
        x[pl.ds(0, HALF), :] = masked_rows(low_rows(core, chips, beside, HALF, HALF), first - HALF, length)
        x[pl.ds(HALF, 2 * HALF), :] = masked_rows(top[...], first, length)
        x[pl.ds(3 * HALF, 2 * HALF), :] = masked_rows(bottom[...], end - 2 * HALF, length)
        x[pl.ds(5 * HALF, HALF), :] = masked_rows(high_rows(core, chips, beside, 0, HALF), end, length)
        depthwise(x, taps, conv, 4 * HALF, HALF, keep=(0, 3 * HALF))
        standardise(conv, taps, (h, s, i), 0, HALF, 0, first, length)
        standardise(conv, taps, (h, s, i), HALF, HALF, HALF, end - HALF, length)

    rows = pl.ds(pl.multiple_of(pl.program_id(0) * HALF, HALF), HALF)
    hidden[...] = h[rows, :]
    standard[...] = s[rows, :]
    inverse[...] = i[rows, :]


SPAN = ROWS + 2 * HALF
FORWARD = (rows_of((SPAN, WIDTH), BF16), rows_of((SPAN, WIDTH), F32), rows_of((SPAN, LANES), F32))


def forward_inner(lengths, frames, taps):
    return pl.pallas_call(
        inner_kernel,
        out_shape=FORWARD,
        in_specs=[SMEM, VMEM, VMEM],
        out_specs=(VMEM, VMEM, VMEM),
        scratch_shapes=[pltpu.VMEM((ROWS, WIDTH), F32), pltpu.VMEM((INNER, WIDTH), F32)],
        compiler_params=LIMIT,
        cost_estimate=pl.CostEstimate(flops=60_000_000, bytes_accessed=4_000_000, transcendentals=800_000),
        name="forward_inner",
    )(lengths, frames, taps)


def fixed(shape, row=0):
    return pl.BlockSpec(shape, lambda i: (row, 0))


SIDE = fixed((3 * HALF, WIDTH))
SCRATCH = [pltpu.VMEM((6 * HALF, WIDTH), F32), pltpu.VMEM((2 * HALF, WIDTH), F32)]
KEPT = [pltpu.VMEM((2 * HALF, WIDTH), BF16), pltpu.VMEM((2 * HALF, WIDTH), F32), pltpu.VMEM((2 * HALF, LANES), F32)]


def forward_edge(lengths, frames, chips, beside, taps, forward):
    def ends(i):
        return (1 + 15 * i, 0)

    return pl.pallas_call(
        edge_kernel,
        grid=(2,),
        out_shape=FORWARD,
        in_specs=[
            SMEM,
            fixed((2 * HALF, WIDTH)),
            fixed((2 * HALF, WIDTH), 7),
            SIDE,
            SIDE,
            fixed((KW + 1, WIDTH)),
            ANY,
            ANY,
            ANY,
        ],
        out_specs=(
            pl.BlockSpec((HALF, WIDTH), ends),
            pl.BlockSpec((HALF, WIDTH), ends),
            pl.BlockSpec((HALF, LANES), ends),
        ),
        scratch_shapes=SCRATCH + KEPT,
        input_output_aliases={6: 0, 7: 1, 8: 2},
        compiler_params=LIMIT,
        cost_estimate=pl.CostEstimate(flops=8_000_000, bytes_accessed=1_000_000, transcendentals=100_000),
        name="forward_edge",
    )(lengths, frames, frames, chips, beside, taps, *forward)


def backward_rows(first, length, upstream, begin, standard, row, inverse, taps, conv_grad, out_row, size, scaled):
    source, rows, held, out = pl.ds(begin, size), pl.ds(row, size), pl.ds(0, size), pl.ds(out_row, size)
    position = first + lax.broadcasted_iota(jnp.int32, (size, 1), 0)
    valid = (position >= 0) & (position < length)
    means, slopes, terms = None, None, []
    for lanes in LANE_BLOCKS:
        value = standard[rows, lanes]
        gain = taps[pl.ds(KW, 1), lanes]
        normal = value * gain
        sigma = 0.5 + 0.5 * jnp.tanh(0.5 * normal)
        grad = jnp.where(valid, upstream[source, lanes] * (sigma + normal * sigma * (1.0 - sigma)), 0.0)
        terms.append(jnp.sum((grad * value).reshape(size // 8, 8, LANES), axis=0))
        grad = grad * gain
        scaled[held, lanes] = grad
        slope = grad * value
        means = grad if means is None else means + grad
        slopes = slope if slopes is None else slopes + slope
    mean = jnp.sum(means, axis=1, keepdims=True) * (1.0 / WIDTH)
    slope = jnp.sum(slopes, axis=1, keepdims=True) * (1.0 / WIDTH)
    scale = inverse[rows, :1]
    for lanes in LANE_BLOCKS:
        value = scaled[held, lanes] - mean - standard[rows, lanes] * slope
        conv_grad[out, lanes] = (scale * value).astype(BF16)
    return terms


def backward_kernel(lengths, upstream, standard, inverse, taps, _, conv_grad, gain_sum, scaled):
    where = where_of(lengths)
    terms = []
    for begin in (0, ROWS // 2):
        span = HALF + begin
        refs = (upstream, span, standard, span, inverse, taps, conv_grad, begin, ROWS // 2, scaled)
        terms.append(backward_rows(where[0] + begin, where[1], *refs))
    for lanes, one, two in zip(LANE_BLOCKS, *terms):
        gain_sum[:, lanes] = one + two


def backward(lengths, upstream, standard, inverse, taps, after):
    return pl.pallas_call(
        backward_kernel,
        out_shape=(rows_of((ROWS, WIDTH), BF16), rows_of((8, WIDTH), F32)),
        in_specs=[SMEM, VMEM, VMEM, VMEM, VMEM, ANY],
        out_specs=(VMEM, VMEM),
        scratch_shapes=[pltpu.VMEM((ROWS // 2, WIDTH), F32)],
        compiler_params=LIMIT,
        cost_estimate=pl.CostEstimate(flops=10_000_000, bytes_accessed=4_000_000, transcendentals=400_000),
        name="backward",
    )(lengths, upstream, standard, inverse, taps, after)


def outer_kernel(lengths, frames, chips, beside, taps, upstream, _, out, x, conv, standard, inverse, scaled):
    where = where_of(lengths)
    first, length, core = where[0], where[1], where[2]
    end = first + ROWS
    top, bottom = frames[pl.ds(0, HALF), :], frames[pl.ds(ROWS - HALF, HALF), :]
    x[pl.ds(0, 2 * HALF), :] = masked_rows(low_rows(core, chips, beside, 0, 2 * HALF), first - 2 * HALF, length)
    x[pl.ds(2 * HALF, HALF), :] = masked_rows(top, first, length)
    x[pl.ds(3 * HALF, HALF), :] = masked_rows(bottom, end - HALF, length)
    x[pl.ds(4 * HALF, 2 * HALF), :] = masked_rows(high_rows(core, chips, beside, 0, 2 * HALF), end, length)
    depthwise(x, taps, conv, 4 * HALF, HALF, keep=(0, 3 * HALF))
    standardise(conv, taps, (None, standard, inverse), 0, 2 * HALF, 0, first, length)
    for row, begin, position in ((0, 0, first - HALF), (HALF, HALF + ROWS, end)):
        refs = (upstream, begin, standard, row, inverse, taps, out, row, HALF, scaled)
        backward_rows(position, length, *refs)


def outer_grads(lengths, frames, chips, beside, taps, upstream, after):
    return pl.pallas_call(
        outer_kernel,
        out_shape=rows_of((2 * HALF, WIDTH), BF16),
        in_specs=[SMEM] + [VMEM] * 5 + [ANY],
        out_specs=VMEM,
        scratch_shapes=SCRATCH + KEPT[1:] + [pltpu.VMEM((HALF, WIDTH), F32)],
        compiler_params=LIMIT,
        cost_estimate=pl.CostEstimate(flops=8_000_000, bytes_accessed=1_000_000, transcendentals=0),
        name="outer_grads",
    )(lengths, frames, chips, beside, taps, upstream, after)


SIDE_LANES = WIDTH // 2


def fill_rows(where, frames, chips, beside, conv_grad, x, g, columns):
    first, length, core = where[0], where[1], where[2]
    low = low_rows(core, chips, beside, HALF, HALF, columns)
    high = high_rows(core, chips, beside, 0, HALF, columns)
    x[pl.ds(0, HALF), :] = masked_rows(low, first - HALF, length)
    x[pl.ds(HALF, ROWS), :] = masked_rows(frames[:, columns], first, length)
    x[pl.ds(HALF + ROWS, HALF), :] = masked_rows(high, first + ROWS, length)
    g[pl.ds(0, 8), :] = jnp.zeros((8, SIDE_LANES), F32)
    g[pl.ds(8, ROWS), :] = conv_grad[:, columns].astype(F32)
    g[pl.ds(8 + ROWS, 8), :] = jnp.zeros((8, SIDE_LANES), F32)


def kernel_grad_lanes(x, g, gain_rows, out, offset):
    chunk = 88

    def lane_block(i, carry):
        lanes = pl.ds(pl.multiple_of(i * LANES, LANES), LANES)
        whole = pl.ds(pl.multiple_of(i * LANES + offset, LANES), LANES)
        sums = [None] * KW
        for begin in range(0, ROWS + 8, chunk):
            x_rows = x[pl.ds(begin, chunk + KW - 8), lanes]
            grad = g[pl.ds(begin, chunk + 8), lanes]
            for shift in range(8):
                moved = grad[8:] if shift == 0 else pltpu.roll(grad, shift, 0)[8:]
                for a in range(KW // 8):
                    j = 8 * a + shift
                    product = (moved * x_rows[8 * a : 8 * a + chunk]).reshape(chunk // 8, 8, LANES)
                    product = jnp.sum(product, axis=0)
                    sums[j] = product if sums[j] is None else sums[j] + product
        out[pl.ds(0, KW), whole] = jnp.concatenate(
            [jnp.sum(value, axis=0, keepdims=True) for value in sums], axis=0
        )
        gain = jnp.sum(gain_rows[:, whole], axis=0, keepdims=True)
        out[pl.ds(KW, 8), whole] = jnp.broadcast_to(gain, (8, LANES))
        return carry

    lax.fori_loop(0, SIDE_LANES // LANES, lane_block, 0)


def first_grad_kernel(lengths, frames, chips, beside, conv_grad, gain_rows, out, x, g):
    where = where_of(lengths)
    fill_rows(where, frames, chips, beside, conv_grad, x, g, pl.ds(0, SIDE_LANES))
    kernel_grad_lanes(x, g, gain_rows, out, 0)


def other_grad_kernel(lengths, frames, chips, beside, conv_grad, gain_rows, first, _, keep, one, two, three, x, g, rows):
    where = where_of(lengths)
    fill_rows(where, frames, chips, beside, conv_grad, x, g, pl.ds(SIDE_LANES, SIDE_LANES))
    rows[pl.ds(0, KW + 8), pl.ds(0, SIDE_LANES)] = first[...]
    kernel_grad_lanes(x, g, gain_rows, rows, SIDE_LANES)
    rows[pl.ds(KW + 8, 8), :] = jnp.zeros((8, WIDTH), F32)
    for step, out in enumerate((keep, one, two, three)):
        columns = pl.ds(pl.multiple_of(lax.rem(where[3] + step, 4) * QUARTER, QUARTER), QUARTER)
        out[...] = rows[:, columns].astype(out.dtype)


GRAD_SCRATCH = [pltpu.VMEM((ROWS + KW, SIDE_LANES), F32), pltpu.VMEM((ROWS + 16, SIDE_LANES), F32)]
GRAD_COST = pl.CostEstimate(flops=25_000_000, bytes_accessed=1_000_000, transcendentals=0)


def kernel_grads_first(lengths, frames, chips, beside, conv_grad, gain_rows):
    return pl.pallas_call(
        first_grad_kernel,
        out_shape=rows_of((KW + 8, SIDE_LANES), F32),
        in_specs=[SMEM] + [VMEM] * 5,
        out_specs=VMEM,
        scratch_shapes=GRAD_SCRATCH,
        compiler_params=LIMIT,
        cost_estimate=GRAD_COST,
        name="kernel_grads_first",
    )(lengths, frames, chips, beside, conv_grad, gain_rows)


def kernel_grads_other(lengths, frames, chips, beside, conv_grad, gain_rows, first, after):
    return pl.pallas_call(
        other_grad_kernel,
        out_shape=(rows_of((MORE, QUARTER), F32),) + (rows_of((MORE, QUARTER), BF16),) * 3,
        in_specs=[SMEM] + [VMEM] * 6 + [ANY],
        out_specs=(VMEM,) * 4,
        scratch_shapes=GRAD_SCRATCH + [pltpu.VMEM((MORE, WIDTH), F32)],
        compiler_params=LIMIT,
        cost_estimate=GRAD_COST,
        name="kernel_grads_other",
    )(lengths, frames, chips, beside, conv_grad, gain_rows, first, after)


def input_grad_kernel(lengths, conv_grad, outer, taps, _, out, token, g):
    where = where_of(lengths)
    token[...] = jnp.zeros(token.shape, F32)
    first, length = where[0], where[1]
    g[pl.ds(0, HALF), :] = outer[pl.ds(0, HALF), :].astype(F32)
    g[pl.ds(HALF, ROWS), :] = conv_grad[...].astype(F32)
    g[pl.ds(HALF + ROWS, HALF), :] = outer[pl.ds(HALF, HALF), :].astype(F32)

    def finish(total, begin):
        return masked_rows(total, first + begin, length).astype(BF16)

    depthwise(g, taps, out, ROWS, 64, finish, {j: KW - j for j in range(1, KW + 1)})


def input_grads(lengths, conv_grad, outer, taps, after):
    return pl.pallas_call(
        input_grad_kernel,
        out_shape=(rows_of((ROWS, WIDTH), BF16), rows_of((8, LANES), F32)),
        in_specs=[SMEM, VMEM, VMEM, VMEM, ANY],
        out_specs=(VMEM, VMEM),
        scratch_shapes=[pltpu.VMEM((ROWS + KW, WIDTH), F32)],
        compiler_params=LIMIT,
        cost_estimate=pl.CostEstimate(flops=50_000_000, bytes_accessed=2_000_000, transcendentals=0),
        name="input_grads",
    )(lengths, conv_grad, outer, taps, after)


def small_call(kernel, name, out_shape, operands, in_specs, scratch=()):
    return pl.pallas_call(
        kernel,
        out_shape=out_shape,
        in_specs=in_specs,
        out_specs=jax.tree.map(lambda _: VMEM, out_shape),
        scratch_shapes=list(scratch),
        compiler_params=LIMIT,
        cost_estimate=pl.CostEstimate(flops=500_000, bytes_accessed=1_500_000, transcendentals=0),
        name=name,
    )(*operands)


def row_products(place, hidden, hidden_other, cot, cot_other, step):
    columns = pl.ds(pl.multiple_of(place[1] * (WIDTH // 2), WIDTH // 2), WIDTH // 2)
    rows = pl.ds(pl.multiple_of(lax.rem(place[0] + step, 4) * QUARTER, QUARTER), QUARTER)
    dims = (((0,), (0,)), ((), ()))
    own_rows = pl.ds(HALF, ROWS)
    return lax.dot_general(
        hidden[own_rows, rows], cot[:, columns], dims, preferred_element_type=F32
    ) + lax.dot_general(hidden_other[own_rows, rows], cot_other[:, columns], dims, preferred_element_type=F32)


def far_kernel(hidden, hidden_other, cot, cot_other, _, far_a, far_b):
    place = place_of()
    value = row_products(place, hidden, hidden_other, cot, cot_other, 2).astype(BF16)
    far_a[...] = value[:, :QUARTER]
    far_b[...] = value[:, QUARTER:]


def far_products(hidden, hidden_other, cot, cot_other, after):
    half = rows_of((QUARTER, QUARTER), BF16)
    operands = (hidden, hidden_other, cot, cot_other, after)
    return small_call(far_kernel, "far_products", (half, half), operands, [VMEM] * 4 + [ANY])


def near_kernel(hidden, hidden_other, cot, cot_other, _, above_a, above_b, below_a, below_b, own):
    place = place_of()
    for step, (a, b) in ((1, (above_a, above_b)), (3, (below_a, below_b))):
        value = row_products(place, hidden, hidden_other, cot, cot_other, step)
        a[...] = value[:, :QUARTER].astype(a.dtype)
        b[...] = value[:, QUARTER:].astype(b.dtype)
    own[...] = row_products(place, hidden, hidden_other, cot, cot_other, 0)


def near_products(hidden, hidden_other, cot, cot_other, after):
    half = (QUARTER, QUARTER)
    shapes = tuple(rows_of(half, dtype) for dtype in (F32, BF16, BF16, F32)) + (rows_of((QUARTER, 2 * QUARTER), F32),)
    operands = (hidden, hidden_other, cot, cot_other, after)
    return small_call(near_kernel, "near_products", shapes, operands, [VMEM] * 4 + [ANY])


def seconds_kernel(above_a, up_a, below_b, down_b, _, second_a, second_b):
    second_a[...] = (above_a[...] + up_a[...].astype(F32)).astype(BF16)
    second_b[...] = (below_b[...] + down_b[...].astype(F32)).astype(BF16)


def seconds(above_a, up_a, below_b, down_b, after):
    return pl.pallas_call(
        seconds_kernel,
        out_shape=(rows_of((QUARTER, QUARTER), BF16),) * 2,
        in_specs=[VMEM, VMEM, VMEM, VMEM, ANY],
        out_specs=(VMEM,) * 2,
        compiler_params=LIMIT,
        cost_estimate=pl.CostEstimate(flops=300_000, bytes_accessed=2_400_000, transcendentals=0),
        name="seconds",
    )(above_a, up_a, below_b, down_b, after)


HALVES = 2 * BLOCK
HELD = (HALVES + EXTRA, WIDTH // 2)


def blocks_kernel(own, down_a, up_a, up_b, down_b, k0, k1, k2, k3, keep, send, total, extra):
    place = place_of()
    core = place[1]
    total[:, :QUARTER] = own[:, :QUARTER] + (down_a[...].astype(F32) + up_a[...].astype(F32))
    total[:, QUARTER:] = own[:, QUARTER:] + (down_b[...].astype(F32) + up_b[...].astype(F32))
    sums = k0[...] + (k1[...].astype(F32) + k2[...].astype(F32) + k3[...].astype(F32))
    extra[...] = jnp.zeros(extra.shape, F32)
    for z in range(2):
        for c in range(2):
            column = (2 * z + c) * BLOCK
            for q in range(5):
                value = sums[8 * q : 8 * q + 8, column : column + BLOCK]
                extra[c, pl.ds(8 * z, 8), pl.ds(q * BLOCK, BLOCK)] = value
    for out, c in ((keep, core), (send, 1 - core)):
        for z in range(2):
            rows = pl.ds(pl.multiple_of((2 * z + c) * BLOCK, BLOCK), BLOCK)
            out[pl.ds(z * BLOCK, BLOCK), :] = total[rows, :].astype(out.dtype)
        out[pl.ds(HALVES, EXTRA), :] = extra[c].astype(out.dtype)


def blocks(own, down_a, up_a, up_b, down_b, rows):
    return small_call(
        blocks_kernel,
        "blocks",
        (rows_of(HELD, F32), rows_of(HELD, BF16)),
        (own, down_a, up_a, up_b, down_b, *rows),
        [VMEM] * 9,
        [pltpu.VMEM((QUARTER, 2 * QUARTER), F32), pltpu.VMEM((2, EXTRA, WIDTH // 2), F32)],
    )


PIECE = BLOCK // 2
PACKED = (PIECE, 4 * (WIDTH // 2) + LANES)
TAIL = pl.ds(4 * (WIDTH // 2), LANES)


def chips_kernel(own, other, keep, send, extra, tail):
    place = place_of()
    z_hi, core, half = place[2], place[1], WIDTH // 2
    more = pl.ds(HALVES, EXTRA)
    extra[...] = own[more, :] + other[more, :].astype(F32)
    for out, z in ((keep, z_hi), (send, 1 - z_hi)):
        for source, c in ((own, core), (other, 1 - core)):
            for i in range(2):
                rows = pl.ds(pl.multiple_of(z * BLOCK + i * PIECE, PIECE), PIECE)
                columns = pl.ds(pl.multiple_of((2 * c + i) * half, half), half)
                out[:, columns] = source[rows, :].astype(out.dtype)
        tail[...] = jnp.zeros(tail.shape, F32)
        rows = pl.ds(pl.multiple_of(8 * z, 8), 8)
        for q in range(5):
            tail[pl.ds(8 * q, 8), pl.ds(0, BLOCK)] = extra[rows, pl.ds(q * BLOCK, BLOCK)]
        out[:, TAIL] = tail[...].astype(out.dtype)


def chip_blocks(own, other):
    return small_call(
        chips_kernel,
        "chip_blocks",
        (rows_of(PACKED, F32), rows_of(PACKED, BF16)),
        (own, other),
        [VMEM, VMEM],
        [pltpu.VMEM((EXTRA, WIDTH // 2), F32), pltpu.VMEM((PIECE, LANES), F32)],
    )


def squares_kernel(mine, other, _, keep, one, two, three, square, extra):
    x, half = lax.axis_index("dp") >> 2, WIDTH // 2
    for block in range(4):
        columns = pl.ds(block * half, half)
        value = mine[:, columns] + other[:, columns].astype(F32)
        square[pl.ds(block % 2 * PIECE, PIECE), pl.ds(block // 2 * half, half)] = value * value
    sums = mine[:, TAIL] + other[:, TAIL].astype(F32)
    extra[...] = sums * sums
    square[pl.ds(BLOCK, EXTRA), :] = jnp.zeros((EXTRA, WIDTH), F32)
    for dp in range(16):
        columns = pl.ds(dp * BLOCK, BLOCK)
        square[pl.ds(BLOCK, 2), columns] = extra[pl.ds(2 * dp, 2), pl.ds(0, BLOCK)]
        square[pl.ds(BLOCK + 2, 1), columns] = extra[pl.ds(KW, 1), pl.ds(0, BLOCK)]
    for step, out in enumerate((keep, one, two, three)):
        columns = pl.ds(pl.multiple_of(lax.rem(x + step, 4) * QUARTER, QUARTER), QUARTER)
        out[...] = square[:, columns].astype(out.dtype)


def squares(mine, other, after):
    shape = (BLOCK + EXTRA, QUARTER)
    return small_call(
        squares_kernel,
        "squares",
        (rows_of(shape, F32),) + (rows_of(shape, BF16),) * 3,
        (mine, other, after),
        [VMEM, VMEM, ANY],
        [pltpu.VMEM((BLOCK + EXTRA, WIDTH), F32), pltpu.VMEM((PIECE, LANES), F32)],
    )


def quarters_kernel(keep, one, two, three, own, out_one, out_two, out_three, parts):
    place = place_of()
    z_lo = place[4]
    total = keep[...] + one[...].astype(F32) + two[...].astype(F32) + three[...].astype(F32)
    for z in range(4):
        parts[lax.rem(z - z_lo + 4, 4)] = total[:, z * BLOCK : (z + 1) * BLOCK]
    for step, out in enumerate((own, out_one, out_two, out_three)):
        out[...] = parts[step].astype(out.dtype)


def quarters(keep, one, two, three):
    shape = (BLOCK + EXTRA, BLOCK)
    return pl.pallas_call(
        quarters_kernel,
        out_shape=(rows_of(shape, F32),) + (rows_of(shape, BF16),) * 3,
        in_specs=[VMEM] * 4,
        out_specs=(VMEM,) * 4,
        scratch_shapes=[pltpu.VMEM((4,) + shape, F32)],
        compiler_params=LIMIT,
        cost_estimate=pl.CostEstimate(flops=1_000_000, bytes_accessed=1_000_000, transcendentals=0),
        name="quarters",
    )(keep, one, two, three)


def means_kernel(own, one, two, three, out, kernel, gain):
    total = own[...] + one[...].astype(F32) + two[...].astype(F32) + three[...].astype(F32)
    total = total * (1.0 / 16)
    out[...] = total[:BLOCK]
    kernel[...] = total[BLOCK : BLOCK + 2]
    gain[...] = total[BLOCK + 2 : BLOCK + 3]


def means(own, one, two, three):
    return pl.pallas_call(
        means_kernel,
        out_shape=(rows_of((BLOCK, BLOCK), F32), rows_of((2, BLOCK), F32), rows_of((1, BLOCK), F32)),
        in_specs=[VMEM] * 4,
        out_specs=(VMEM,) * 3,
        compiler_params=LIMIT,
        cost_estimate=pl.CostEstimate(flops=100_000, bytes_accessed=200_000, transcendentals=0),
        name="means",
    )(own, one, two, three)


def on_device(frames_in, cotangent, lengths, out_weight, conv_kernel, layer_norm_gain):
    seq = lax.axis_index("seq")
    core = seq % 2
    frames, cot = frames_in[0], cotangent[0]
    row = lax.broadcasted_iota(jnp.int32, (KW + 1, WIDTH), 0)
    taps = jnp.where(row < KW, jnp.pad(conv_kernel, ((0, 1), (0, 0))), layer_norm_gain[None])
    begin = jnp.concatenate([frames[: 2 * HALF], cot[:HALF]], axis=0)
    end = jnp.concatenate([frames[-2 * HALF :], cot[-HALF:]], axis=0)
    chips = move_neighbour(jnp.where(core == 0, begin, end))
    beside = move_core(jnp.where(core == 0, end, begin))
    cot_other = move_core(cot)
    forward = forward_inner(lengths, frames, taps)
    hidden, standard, inverse = forward_edge(lengths, frames, chips, beside, taps, forward)
    hidden_other = move_core(hidden)
    low = jnp.where(core == 0, chips[2 * HALF :], beside[2 * HALF :])
    high = jnp.where(core == 0, beside[2 * HALF :], chips[2 * HALF :])
    late_cot, _ = lax.optimization_barrier((jnp.concatenate([low, cot, high], axis=0), hidden))
    upstream = lax.dot_general(late_cot, out_weight, (((1,), (1,)), ((), ())), preferred_element_type=F32)
    operands = (hidden, hidden_other, cot, cot_other)
    far_a, far_b = far_products(*operands, upstream)
    above_a, above_b, below_a, below_b, own = near_products(*operands, far_a)
    up_a = move_y(far_a, 1)
    down_b = move_y(far_b, -1)
    up_b = move_y(above_b, 1)
    down_a = move_y(below_a, -1)
    conv_grad, gain_rows = backward(lengths, upstream, standard, inverse, taps, own)
    operands = (lengths, frames, chips, beside, conv_grad, gain_rows)
    rows = kernel_grads_first(*operands)
    second_a, second_b = seconds(above_a, up_a, below_b, down_b, rows)
    up_a = move_y(second_a, 1)
    down_b = move_y(second_b, -1)
    rows = kernel_grads_other(*operands, rows, second_a)
    rows = [rows[0]] + [move_y(rows[k], k) for k in (1, 2, 3)]
    own, other = blocks(own, down_a, up_a, up_b, down_b, rows)
    own, other = chip_blocks(own, move_core(other))
    outer = outer_grads(lengths, frames, chips, beside, taps, upstream, other)
    input_grad, token = input_grads(lengths, conv_grad, outer, taps, other)
    keep, *sent = squares(own, move_z_hi(other), token)
    keep, *sent = quarters(keep, *(move_x(value, k + 1) for k, value in enumerate(sent)))
    out, kernel, gain = means(keep, *(move_z_lo(value, k + 1) for k, value in enumerate(sent)))
    return input_grad[None], out, kernel, gain[0]


def solution(mesh):
    return jax.shard_map(
        on_device,
        mesh=mesh,
        in_specs=(P("dp", "seq", None), P("dp", "seq", None), P("dp"), P(), P(), P()),
        out_specs=(P("dp", "seq", None), P("seq", "dp"), P("dp", "seq"), P("seq")),
        check_vma=False,
    )
```
